128 devices in a mesh: row: 8 (over x, z_lo), col: 16 (over z_hi, y, core).
Axes of the slice: x: 4, y: 4, z: 4 (z_hi: 2, z_lo: 2; z = z_hi * 2 + z_lo), core: 2. Of those that a mesh axis runs over, the one named last changes fastest.
Arguments:
- inputs: bfloat16 [1024, 8192], P('row', 'col'), may hold values from -6 to 6
- gate_weight: bfloat16 [8192, 16384], P('col', 'row'), may hold values from -0.0625 to 0.0625
- up_weight: bfloat16 [8192, 16384], P('col', 'row'), may hold values from -0.0625 to 0.0625
- down_weight: bfloat16 [16384, 8192], P('row', 'col'), may hold values from -0.046875 to 0.046875
- out_grad: bfloat16 [1024, 8192], P('row', 'col'), may hold values from -1.5 to 1.5
Outputs:
- mixed: bfloat16 [1024, 8192], P('row', 'col')
- grad_input: bfloat16 [1024, 8192], P('row', 'col')
- grad_gate: float32 [8192, 16384], P('col', 'row')
- grad_up: float32 [8192, 16384], P('col', 'row')
- grad_down: float32 [16384, 8192], P('row', 'col')
The draws below stay inside these ranges and needn't reach their ends.
All inputs are finite; a program needn't handle non-finite values.
Results may differ from the reference program's by a relative error of at most 0.033.
Values may be sent and summed in bfloat16 or wider, within the bound.
A program may use at most 128 MiB of HBM per device.

```python
import jax
import jax.numpy as jnp
from jax import lax

D = 8192
FF = 16384
TOKENS = 1024
N_COL = 16


def block_scale(stream_key, shape, pieces, low, top_value):
    level = 1.0
    for axis_at, parts in pieces:
        steps = jax.random.uniform(jax.random.fold_in(jax.random.fold_in(stream_key, 6), axis_at), (parts,), jnp.float32, low / len(pieces), top_value / len(pieces))
        level = level * jnp.repeat(jnp.exp(steps), shape[axis_at] // parts).reshape((-1,) + (1,) * (len(shape) - 1 - axis_at))
    return level


def centred(own_key, shape, scale, most, cuts=(), dtype=jnp.bfloat16):
    gain = block_scale(own_key, shape, cuts, -0.22, 0.18) if cuts else 1.0
    values = jax.random.normal(own_key, shape, jnp.float32) * scale * gain
    return jnp.minimum(jnp.maximum(values, -most), most).astype(dtype)


def setup_inputs(seed: int = 0) -> dict:
    splits = jax.random.split(jax.random.key(seed), 6)
    return {
        "inputs": centred(splits[0], (TOKENS, D), 1.0, 6.0, ((0, 8), (1, 16))),
        "gate_weight": centred(splits[1], (D, FF), D ** -0.5, 0.0625, ((0, 16), (1, 8))),
        "up_weight": centred(splits[2], (D, FF), D ** -0.5, 0.0625, ((0, 16), (1, 8))),
        "down_weight": centred(splits[3], (FF, D), FF ** -0.5, 0.046875, ((0, 8), (1, 16))),
        "out_grad": centred(splits[4], (TOKENS, D), 0.25, 1.5, ((0, 8), (1, 16))),
    }


def silu_parts(gate):
    sig = jax.nn.sigmoid(gate)
    return gate * sig, sig * (1.0 + gate * (1.0 - sig))


def rounded(term):
    return lax.optimization_barrier(term.astype(jnp.bfloat16)).astype(jnp.float32)


def reference(inputs, gate_weight, up_weight, down_weight, out_grad):
    width = D // N_COL
    gate = jnp.zeros((TOKENS, FF), jnp.float32)
    up = jnp.zeros((TOKENS, FF), jnp.float32)
    act_grad = jnp.zeros((TOKENS, FF), jnp.float32)
    for block in range(N_COL):
        lower = block * width
        upper = lower + width
        part_x = inputs[:, lower:upper]
        gate = gate + rounded(jnp.dot(part_x, gate_weight[lower:upper], preferred_element_type=jnp.float32))
        up = up + rounded(jnp.dot(part_x, up_weight[lower:upper], preferred_element_type=jnp.float32))
        act_grad = act_grad + rounded(jnp.dot(out_grad[:, lower:upper], down_weight[:, lower:upper].T, preferred_element_type=jnp.float32))
    act, slope = silu_parts(gate)
    hidden = (act * up).astype(jnp.bfloat16)
    mixed = jnp.dot(hidden, down_weight, preferred_element_type=jnp.float32).astype(jnp.bfloat16)
    grad_down = jnp.dot(hidden.T, out_grad, preferred_element_type=jnp.float32)
    grad_gate_act = (act_grad * up * slope).astype(jnp.bfloat16)
    grad_up_act = (act_grad * act).astype(jnp.bfloat16)
    grad_gate = jnp.dot(inputs.T, grad_gate_act, preferred_element_type=jnp.float32)
    grad_up = jnp.dot(inputs.T, grad_up_act, preferred_element_type=jnp.float32)
    grad_input = jnp.dot(grad_gate_act, gate_weight.T, preferred_element_type=jnp.float32)
    grad_input = grad_input + jnp.dot(grad_up_act, up_weight.T, preferred_element_type=jnp.float32)
    return mixed, grad_input.astype(jnp.bfloat16), grad_gate, grad_up, grad_down
```

```python
import functools

import jax
import jax.numpy as jnp
from jax import lax
from jax.experimental import pallas as pl
from jax.experimental.pallas import tpu as pltpu
from jax.sharding import PartitionSpec as P

MESH = pl.DeviceIdType.MESH
BF16, F32 = jnp.bfloat16, jnp.float32
CHUNKS = 4
NN = (((1,), (0,)), ((), ()))
NT = (((1,), (1,)), ((), ()))
TN = (((0,), (0,)), ((), ()))


def dot(left, right, dims):
    return lax.dot_general(left, right, dims, preferred_element_type=F32)


def silu_parts(gate):
    sig = jax.nn.sigmoid(gate)
    return gate * sig, sig * (1.0 + gate * (1.0 - sig))


def kernel(
    x_hbm, og_hbm, wg_hbm, wu_hbm, wd_hbm,
    h_out, gg_out, ug_out, xf_out, of_out, mix_out, gi_out,
    xo, wg, wu, wd, part, core_in, y1b, y2b, zb, za, y1a, y2a, full, mix, mix_x, mix_z, outs,
    send_sem, recv_sem, load_sem, weight_sem, store_sem, out_sem,
):
    row, col = lax.axis_index("row"), lax.axis_index("col")
    x, zl = row // 2, row % 2
    zh, y, core = col // 8, (col // 2) % 4, col % 2
    zo, other = 1 - zh, 1 - core
    y_next, y_prev, y_far = (y + 1) % 4, (y + 3) % 4, (y + 2) % 4
    rows, width = x_hbm.shape
    step = rows // CHUNKS
    hidden = wg_hbm.shape[1]
    half = hidden // 2

    def device(x=x, zl=zl, zh=zh, y=y, core=core):
        return {"row": x * 2 + zl, "col": zh * 8 + y * 2 + core}

    to_core = device(core=other)
    to_next, to_prev = device(y=y_next), device(y=y_prev)
    to_zh, to_zl = device(zh=zo), device(zl=1 - zl)
    to_x = [device(x=(x + d) % 4) for d in (1, 2, 3)]
    from_x = [(x + 4 - d) % 4 for d in (1, 2, 3)]

    pending = []
    slots = {}

    def remote(name, j, src, dst, target):
        k = slots.setdefault(name, len(slots))
        return pltpu.make_async_remote_copy(
            src_ref=src, dst_ref=dst, send_sem=send_sem.at[k, j], recv_sem=recv_sem.at[k, j],
            device_id=target, device_id_type=MESH,
        )

    def send(name, j, src, dst, target):
        copy = remote(name, j, src, dst, target)
        copy.start()
        pending.append(copy)

    def arrive(name, j, dst):
        remote(name, j, dst, dst, to_core).wait_recv()

    weights = []
    for i, (src, dst) in enumerate(((wg_hbm, wg), (wu_hbm, wu), (wd_hbm, wd))):
        weights.append(pltpu.make_async_copy(src, dst, weight_sem.at[i]))
    loads = []
    for j in range(CHUNKS):
        for i, src in enumerate((x_hbm, og_hbm)):
            loads.append(
                pltpu.make_async_copy(
                    src.at[pl.ds(j * step, step)], xo.at[j, x, zl, i], load_sem.at[i, j]
                )
            )
    for copy in loads + weights:
        copy.start()

    barrier = pltpu.get_barrier_semaphore()
    peers = [to_core, to_next, to_prev, to_zh, to_zl] + to_x
    for peer in peers:
        pl.semaphore_signal(barrier, inc=1, device_id=peer, device_id_type=MESH)
    pl.semaphore_wait(barrier, len(peers))

    def gather_own(j):
        loads[2 * j].wait()
        loads[2 * j + 1].wait()
        mine = xo.at[j, x, zl]
        send("row_z", j, mine, mine, to_zl)
        for d in range(3):
            send(f"row_x{d}", j, mine, mine, to_x[d])

    def gather_pair(j):
        theirs = xo.at[j, x, 1 - zl]
        arrive("row_z", j, theirs)
        for d in range(3):
            send(f"row_xz{d}", j, theirs, theirs, to_x[d])

    stores = []

    def store(src, dst, a, j):
        copy = pltpu.make_async_copy(src, dst, store_sem.at[a, j])
        copy.start()
        stores.append(copy)

    def products(j):
        for d in range(3):
            arrive(f"row_x{d}", j, xo.at[j, from_x[d], zl])
            arrive(f"row_xz{d}", j, xo.at[j, from_x[d], 1 - zl])
        for a, (w, i, dims) in enumerate(((wg, 0, NN), (wu, 0, NN), (wd, 1, NT))):
            if j == 0:
                weights[a].wait()
            left = xo[j, :, :, i].reshape(8 * step, width)
            for t in range(2):
                cols = slice(t * half, (t + 1) * half)
                right = w[:, cols] if dims == NN else w[cols, :]
                value = dot(left, right, dims).astype(BF16)
                part[j, :, :, :, a, :, cols] = value.reshape(2, 4, 2, 16, half)
            send(f"core_in{a}", j, part.at[j, other, :, :, a], core_in.at[j, :, :, a], to_core)
        store(xo.at[j, :, :, 0], xf_out.at[j], 0, j)
        store(xo.at[j, :, :, 1], of_out.at[j], 1, j)

    def core_sum(j):
        for a in range(3):
            arrive(f"core_in{a}", j, core_in.at[j, :, :, a])
        pair = slice(0, 2)

        def add(yy, zz, arrays):
            part[j, core, yy, zz, arrays] += core_in[j, yy, zz, arrays]

        for z in range(2):
            add(y_far, z, pair)
        send("y1b+", j, part.at[j, core, y_far, 0, pair], y1b.at[j, 0], to_next)
        send("y1b-", j, part.at[j, core, y_far, 1, pair], y1b.at[j, 1], to_prev)
        for yy in range(4):
            add(yy, zo, 2)
        send("za", j, part.at[j, core, :, zo, 2], za.at[j], to_zh)
        add(y_next, 1, pair)
        send("y2b+e", j, part.at[j, core, y_next, 1, pair], y2b.at[j, 0, 1], to_next)
        add(y_prev, 0, pair)
        send("y2b-e", j, part.at[j, core, y_prev, 0, pair], y2b.at[j, 1, 0], to_prev)
        add(y_next, 0, pair)
        add(y_prev, 1, pair)
        add(y, 0, pair)
        add(y, 1, pair)
        for yy in range(4):
            add(yy, zh, 2)

    low, high = slice(0, half), slice(half, hidden)

    def first_sum(j):
        pair = slice(0, 2)
        arrive("y1b+", j, y1b.at[j, 0])
        part[j, core, y_next, 0, pair] += y1b[j, 0]
        send("y2b+l", j, part.at[j, core, y_next, 0, pair], y2b.at[j, 0, 0], to_next)
        arrive("y1b-", j, y1b.at[j, 1])
        part[j, core, y_prev, 1, pair] += y1b[j, 1]
        send("y2b-l", j, part.at[j, core, y_prev, 1, pair], y2b.at[j, 1, 1], to_prev)
        arrive("za", j, za.at[j])
        part[j, core, y_far, zh, 2] += za[j, y_far]
        send("y1a+", j, part.at[j, core, y_far, zh, 2, :, low], y1a.at[j, 0], to_next)
        send("y1a-", j, part.at[j, core, y_far, zh, 2, :, high], y1a.at[j, 1], to_prev)
        part[j, core, y_next, zh, 2] += za[j, y_next]
        send("y2a+e", j, part.at[j, core, y_next, zh, 2, :, high], y2a.at[j, 0, :, high], to_next)
        part[j, core, y_prev, zh, 2] += za[j, y_prev]
        send("y2a-e", j, part.at[j, core, y_prev, zh, 2, :, low], y2a.at[j, 1, :, low], to_prev)

    def second_sum(j):
        pair = slice(0, 2)
        arrive("y1a+", j, y1a.at[j, 0])
        part[j, core, y_next, zh, 2, :, low] += y1a[j, 0]
        send("y2a+l", j, part.at[j, core, y_next, zh, 2, :, low], y2a.at[j, 0, :, low], to_next)
        arrive("y1a-", j, y1a.at[j, 1])
        part[j, core, y_prev, zh, 2, :, high] += y1a[j, 1]
        send("y2a-l", j, part.at[j, core, y_prev, zh, 2, :, high], y2a.at[j, 1, :, high], to_prev)
        arrive("y2b+e", j, y2b.at[j, 0, 1])
        arrive("y2b+l", j, y2b.at[j, 0, 0])
        arrive("y2b-e", j, y2b.at[j, 1, 0])
        arrive("y2b-l", j, y2b.at[j, 1, 1])
        total = part[j, core, y, zo, pair].astype(F32) + y2b[j, 0, zo].astype(F32)
        part[j, core, y, zo, pair] = (total + y2b[j, 1, zo].astype(F32)).astype(BF16)
        send("zb", j, part.at[j, core, y, zo, pair], zb.at[j], to_zh)

    def activations(j):
        arrive("y2a+e", j, y2a.at[j, 0, :, high])
        arrive("y2a+l", j, y2a.at[j, 0, :, low])
        arrive("y2a-e", j, y2a.at[j, 1, :, low])
        arrive("y2a-l", j, y2a.at[j, 1, :, high])
        arrive("zb", j, zb.at[j])
        tile = hidden // 4
        for t in range(4):
            cols = slice(t * tile, (t + 1) * tile)

            def term(*refs):
                total = refs[0].astype(F32)
                for ref in refs[1:]:
                    total = total + ref.astype(F32)
                return total

            gate, up = (
                term(
                    part[j, core, y, zh, a, :, cols], y2b[j, 0, zh, a, :, cols],
                    y2b[j, 1, zh, a, :, cols], zb[j, a, :, cols],
                )
                for a in range(2)
            )
            act_grad = term(
                part[j, core, y, zh, 2, :, cols], za[j, y, :, cols],
                y2a[j, 0, :, cols], y2a[j, 1, :, cols],
            )
            act, slope = silu_parts(gate)
            full[j, core, y, zh, 0, :, cols] = (act * up).astype(BF16)
            full[j, core, y, zh, 1, :, cols] = (act_grad * up * slope).astype(BF16)
            full[j, core, y, zh, 2, :, cols] = (act_grad * act).astype(BF16)
        mine, last = full.at[j, core, y, zh, pl.ds(0, 2)], full.at[j, core, y, zh, 2]
        send("gzb", j, mine, mine, to_zh)
        send("gyb+o", j, mine, mine, to_next)
        send("gyb-o", j, mine, mine, to_prev)
        send("gya+", j, last, last, to_next)
        send("gya-", j, last, last, to_prev)
        send("gza_o", j, last, last, to_zh)
        own = full.at[j, core, y, zh]
        send("gc_o", j, own, own, to_core)

    def spread_z(j):
        theirs = full.at[j, core, y, zo, pl.ds(0, 2)]
        arrive("gzb", j, theirs)
        send("gyb+z", j, theirs, theirs, to_next)
        send("gyb-z", j, theirs, theirs, to_prev)
        send("gc_z", j, theirs, theirs, to_core)
        for name, yy, cols, target in (("+", y_prev, low, to_next), ("-", y_next, high, to_prev)):
            piece = full.at[j, core, yy, zh, 2]
            arrive("gya" + name, j, piece)
            send("gfa" + name, j, piece.at[:, cols], piece.at[:, cols], target)
            send("gza" + name, j, piece, piece, to_zh)
            send("gca" + name, j, piece, piece, to_core)

    def spread_y(j):
        pair = pl.ds(0, 2)
        for name, yy, z, target in (("+", y_prev, 0, to_next), ("-", y_next, 1, to_prev)):
            arrive(f"gyb{name}o", j, full.at[j, core, yy, zh, pair])
            arrive(f"gyb{name}z", j, full.at[j, core, yy, zo, pair])
            piece = full.at[j, core, yy, z, pair]
            send("gfb" + name, j, piece, piece, target)
            both = full.at[j, core, yy, :, pair]
            send("gcb" + name, j, both, both, to_core)
        far = full.at[j, core, y_far, zh, 2]
        arrive("gfa+", j, far.at[:, low])
        arrive("gfa-", j, far.at[:, high])
        send("gza_f", j, far, far, to_zh)
        send("gca_f", j, far, far, to_core)

    def spread_core(j):
        pair = pl.ds(0, 2)
        arrive("gfb+", j, full.at[j, core, y_far, 0, pair])
        arrive("gfb-", j, full.at[j, core, y_far, 1, pair])
        both = full.at[j, core, y_far, :, pair]
        send("gcb_f", j, both, both, to_core)
        arrive("gza_o", j, full.at[j, core, y, zo, 2])
        arrive("gza+", j, full.at[j, core, y_prev, zo, 2])
        arrive("gza-", j, full.at[j, core, y_next, zo, 2])
        arrive("gza_f", j, full.at[j, core, y_far, zo, 2])
        rest = full.at[j, core, :, zo, 2]
        send("gca_z", j, rest, rest, to_core)

    def outputs(j):
        pair = pl.ds(0, 2)
        arrive("gc_o", j, full.at[j, other, y, zh])
        arrive("gc_z", j, full.at[j, other, y, zo, pair])
        arrive("gca+", j, full.at[j, other, y_prev, zh, 2])
        arrive("gca-", j, full.at[j, other, y_next, zh, 2])
        arrive("gcb+", j, full.at[j, other, y_prev, :, pair])
        arrive("gcb-", j, full.at[j, other, y_next, :, pair])
        arrive("gca_f", j, full.at[j, other, y_far, zh, 2])
        arrive("gcb_f", j, full.at[j, other, y_far, :, pair])
        arrive("gca_z", j, full.at[j, other, :, zo, 2])
        for a, dst in enumerate((h_out, gg_out, ug_out)):
            store(full.at[j, :, :, :, a], dst.at[j], 2 + a, j)
        h, gg, ug = (full[j, :, :, :, a].reshape(8 * step, hidden) for a in range(3))
        shape = (4, 2, step, width)
        mix[j, :, :, 0] = dot(h, wd[...], NN).astype(BF16).reshape(shape)
        total = dot(gg, wg[...], NT) + dot(ug, wu[...], NT)
        mix[j, :, :, 1] = total.astype(BF16).reshape(shape)
        for d in range(3):
            send(f"mix_x{d}", j, mix.at[j, (x + d + 1) % 4], mix_x.at[j, d], to_x[d])

    def row_sum(j):
        for d in range(3):
            arrive(f"mix_x{d}", j, mix_x.at[j, d])

        def total(z):
            value = mix[j, x, z].astype(F32)
            for d in range(3):
                value = value + mix_x[j, d, z].astype(F32)
            return value

        mix[j, x, 1 - zl] = total(1 - zl).astype(BF16)
        send("mix_z", j, mix.at[j, x, 1 - zl], mix_z.at[j], to_zl)

    def finish(j):
        value = mix[j, x, zl].astype(F32)
        for d in range(3):
            value = value + mix_x[j, d, zl].astype(F32)
        arrive("mix_z", j, mix_z.at[j])
        outs[:, j] = (value + mix_z[j].astype(F32)).astype(BF16)

    stages = [products, core_sum, first_sum, second_sum, activations, spread_z, spread_y, spread_core, outputs, row_sum, finish]
    gather_own(0)
    gather_pair(0)
    gather_own(1)
    gather_pair(1)
    for t in range(2 * (CHUNKS - 1) + len(stages)):
        for j in range(CHUNKS):
            if 0 <= t - 2 * j < len(stages):
                stages[t - 2 * j](j)
        if t == 0 or t == 2:
            gather_own(2 + t // 2)
            gather_pair(2 + t // 2)

    final = [
        pltpu.make_async_copy(outs.at[i], dst, out_sem.at[i])
        for i, dst in enumerate((mix_out, gi_out))
    ]
    for copy in final:
        copy.start()
    for copy in pending:
        copy.wait_send()
    for copy in stores + final:
        copy.wait()


def exchange(inputs, gate_weight, up_weight, down_weight, out_grad):
    rows, width = inputs.shape
    hidden = gate_weight.shape[1]
    step = rows // CHUNKS

    def buffer(*shape):
        return pltpu.VMEM(shape, BF16)

    def out(*shape):
        return jax.ShapeDtypeStruct(shape, BF16)

    wide = out(CHUNKS, 2, 4, 2, 16, hidden)
    thin = out(CHUNKS, 4, 2, step, width)
    kinds = 56
    any_space = pl.BlockSpec(memory_space=pl.ANY)
    return pl.pallas_call(
        kernel,
        out_shape=(wide, wide, wide, thin, thin, out(CHUNKS, step, width), out(CHUNKS, step, width)),
        in_specs=[any_space] * 5,
        out_specs=[any_space] * 7,
        scratch_shapes=[
            buffer(CHUNKS, 4, 2, 2, step, width),
            buffer(width, hidden),
            buffer(width, hidden),
            buffer(hidden, width),
            buffer(CHUNKS, 2, 4, 2, 3, 16, hidden),
            buffer(CHUNKS, 4, 2, 3, 16, hidden),
            buffer(CHUNKS, 2, 2, 16, hidden),
            buffer(CHUNKS, 2, 2, 2, 16, hidden),
            buffer(CHUNKS, 2, 16, hidden),
            buffer(CHUNKS, 4, 16, hidden),
            buffer(CHUNKS, 2, 16, hidden // 2),
            buffer(CHUNKS, 2, 16, hidden),
            buffer(CHUNKS, 2, 4, 2, 3, 16, hidden),
            buffer(CHUNKS, 4, 2, 2, step, width),
            buffer(CHUNKS, 3, 2, 2, step, width),
            buffer(CHUNKS, 2, step, width),
            buffer(2, CHUNKS, step, width),
            pltpu.SemaphoreType.DMA((kinds, CHUNKS)),
            pltpu.SemaphoreType.DMA((kinds, CHUNKS)),
            pltpu.SemaphoreType.DMA((2, CHUNKS)),
            pltpu.SemaphoreType.DMA((3,)),
            pltpu.SemaphoreType.DMA((5, CHUNKS)),
            pltpu.SemaphoreType.DMA((2,)),
        ],
        compiler_params=pltpu.CompilerParams(
            collective_id=0, has_side_effects=True, vmem_limit_bytes=60 << 20
        ),
    )(inputs, out_grad, gate_weight, up_weight, down_weight)


def weight_kernel(tiles, x, og, gg, ug, h, grad_gate, grad_up, grad_down):
    i = pl.program_id(0)

    @pl.when(i < tiles)
    def _():
        grad_gate[...] = dot(x[...], gg[...], TN)

    @pl.when((i >= tiles) & (i < 2 * tiles))
    def _():
        grad_up[...] = dot(x[...], ug[...], TN)

    @pl.when(i >= 2 * tiles)
    def _():
        grad_down[...] = dot(h[...], og[...], TN)


def weight_grads(x, og, gg, ug, h):
    tokens, width = x.shape
    hidden = h.shape[1]
    tiles = 4
    tile = hidden // tiles

    def at(phase):
        return lambda i: jnp.clip(i - phase * tiles, 0, tiles - 1)

    def cols(phase):
        place = at(phase)
        return lambda i: (0, place(i))

    whole = pl.BlockSpec((tokens, width), lambda i: (0, 0))
    down = at(2)
    return pl.pallas_call(
        functools.partial(weight_kernel, tiles),
        grid=(3 * tiles,),
        out_shape=(
            jax.ShapeDtypeStruct((width, hidden), F32),
            jax.ShapeDtypeStruct((width, hidden), F32),
            jax.ShapeDtypeStruct((hidden, width), F32),
        ),
        in_specs=[whole, whole] + [pl.BlockSpec((tokens, tile), cols(p)) for p in range(3)],
        out_specs=[
            pl.BlockSpec((width, tile), cols(0)),
            pl.BlockSpec((width, tile), cols(1)),
            pl.BlockSpec((tile, width), lambda i: (down(i), 0)),
        ],
        compiler_params=pltpu.CompilerParams(vmem_limit_bytes=48 << 20),
    )(x, og, gg, ug, h)


def body(inputs, gate_weight, up_weight, down_weight, out_grad):
    h, gg, ug, x, og, mixed, grad_input = exchange(
        inputs, gate_weight, up_weight, down_weight, out_grad
    )
    rows, width = inputs.shape
    hidden = gate_weight.shape[1]
    grad_gate, grad_up, grad_down = weight_grads(
        x.reshape(-1, width), og.reshape(-1, width),
        gg.reshape(-1, hidden), ug.reshape(-1, hidden), h.reshape(-1, hidden),
    )
    return mixed.reshape(rows, width), grad_input.reshape(rows, width), grad_gate, grad_up, grad_down


def solution(mesh):
    in_specs = (P("row", "col"), P("col", "row"), P("col", "row"), P("row", "col"), P("row", "col"))
    out_specs = (
        P("row", "col"),
        P("row", "col"),
        P("col", "row"),
        P("col", "row"),
        P("row", "col"),
    )
    return jax.shard_map(body, mesh=mesh, in_specs=in_specs, out_specs=out_specs, check_vma=False)
```

```python
import functools

import jax
import jax.numpy as jnp
from jax import lax
from jax.experimental import pallas as pl
from jax.experimental.pallas import tpu as pltpu
from jax.sharding import PartitionSpec as P

MESH = pl.DeviceIdType.MESH
BF16, F32 = jnp.bfloat16, jnp.float32
PARTIAL = BF16
OFFSETS = ((0, 0), (0, 1), (2, 0), (1, 1), (3, 1), (2, 1), (1, 0), (3, 0))
CHUNKS = len(OFFSETS)
PAIR = OFFSETS.index((0, 1))
LATE = 2
COPIES = 260
NN = (((1,), (0,)), ((), ()))
NT = (((1,), (1,)), ((), ()))
TN = (((0,), (0,)), ((), ()))


def dot(left, right, dims):
    return lax.dot_general(left, right, dims, preferred_element_type=F32)


def silu_parts(gate):
    sig = jax.nn.sigmoid(gate)
    return gate * sig, sig * (1.0 + gate * (1.0 - sig))


ORDER = (
    ("R0", 0), ("G", 0), ("U", 0), ("R1", 0), ("A", 0), ("CB", 0), ("CA", 0), ("G", 6), ("U", 6), ("G", 1),
    ("FB+", 0), ("FB-", 0), ("U", 1), ("CB", 6), ("G", 2), ("A", 1), ("CB", 1), ("P0", 0), ("A", 6), ("FA", 0),
    ("SB", 0), ("FB+", 6), ("FB-", 6), ("A", 7), ("P1", 0), ("U", 2), ("CA", 6), ("G", 7), ("FB+", 1), ("FB-", 1),
    ("CB", 2), ("CA", 7), ("CA", 1), ("G", 3), ("SA+", 0), ("SA-", 0), ("U", 3), ("G", 4), ("SB", 6), ("U", 4),
    ("CB", 3), ("FA", 6), ("G", 5), ("FB-", 2), ("SB", 1), ("A", 3), ("A", 4), ("FA", 7), ("FB+", 2), ("U", 7),
    ("FB+", 3), ("FB-", 3), ("CA", 3), ("CA", 4), ("CB", 4), ("FA", 1), ("CB", 7), ("SA-", 6), ("SA+", 7),
    ("SA+", 6), ("A", 2), ("A", 5), ("SA-", 7), ("SB", 2), ("U", 5), ("SB", 3), ("CA", 5), ("CA", 2), ("FB+", 4),
    ("FB-", 4), ("FA", 3), ("CB", 5), ("SA+", 1), ("SA-", 1), ("FA", 4), ("FB-", 7), ("FB+", 7), ("SB", 4),
    ("SA-", 3), ("SA+", 3), ("FA", 5), ("FB+", 5), ("FB-", 5), ("FA", 2), ("SA+", 4), ("SA-", 4), ("SB", 7),
    ("ACT", 3), ("SA-", 5), ("SA+", 5), ("SB", 5), ("SA-", 2), ("SA+", 2), ("YA+", 3), ("YA-", 3), ("ACT", 7),
    ("ZB", 3), ("ACT", 2), ("ZF", 3), ("YA-", 7), ("YA+", 7), ("ZB", 7), ("YB-", 3), ("YB+", 3), ("ACT", 6),
    ("YA+", 2), ("YA-", 2), ("ZB", 2), ("ZF", 7), ("ZA", 3), ("YB+", 7), ("YB-", 7), ("ACT", 4), ("ZB", 6),
    ("MIX", 3), ("YA-", 6), ("YA+", 6), ("YF", 3), ("ZF", 2), ("ZA", 7), ("GI", 3), ("YB+", 2), ("YB-", 2),
    ("ACT", 5), ("ZB", 4), ("MIX", 7), ("YA-", 4), ("YA+", 4), ("YF", 7), ("ZA", 2), ("GI", 7), ("YB-", 6),
    ("ZB", 5), ("ZF", 6), ("YB+", 6), ("MIX", 2), ("YF", 2), ("YA-", 5), ("YA+", 5), ("GI", 2), ("YB+", 4),
    ("YB-", 4), ("ACT", 1), ("ZF", 4), ("ZA", 6), ("YB+", 5), ("MIX", 6), ("YF", 6), ("ZF", 5), ("YB-", 5),
    ("ACT", 0), ("YF", 4), ("ZB", 1), ("GI", 6), ("YA-", 1), ("YA+", 1), ("GI", 4), ("ZA", 4), ("YF", 5),
    ("YA+", 0), ("YA-", 0), ("MIX", 4), ("GI", 5), ("ZA", 5), ("YB-", 1), ("YB+", 1), ("ZB", 0), ("ZF", 1),
    ("ZF", 0), ("MIX", 5), ("W", 0), ("W", 0), ("W", 0), ("W", 0), ("YF", 1), ("W", 0), ("YB+", 0), ("YB-", 0),
    ("W", 0), ("GI", 1), ("ZA", 1), ("RS1", 0), ("W", 0), ("ZA", 0), ("MIX", 1), ("YF", 0), ("RS0", 0), ("MIX", 0),
    ("W", 0), ("GI", 0), ("W", 0), ("W", 0), ("FI1", 0), ("W", 0), ("W", 0), ("FI0", 0),
)


def kernel(
    x_hbm, og_hbm, wg_hbm, wu_hbm, wd_hbm,
    h_out, gg_out, ug_out, xf_out, of_out, mix_out, gi_out, gate_out, up_out, down_out,
    xo, wg, wu, wd, part, core_in, y1b, y2b, zb, za, y1a, y2a, full, mix, mix_in, mix_z, outs, wide_tiles, tall_tiles,
    send_sem, recv_sem, load_sem, weight_sem, store_sem, tile_sem, out_sem,
):
    row, col = lax.axis_index("row"), lax.axis_index("col")
    x, zl = row // 2, row % 2
    zh, y, core = col // 8, (col // 2) % 4, col % 2
    zo, other = 1 - zh, 1 - core
    y_next, y_prev, y_far = (y + 1) % 4, (y + 3) % 4, (y + 2) % 4
    rows, width = x_hbm.shape
    hidden = wg_hbm.shape[1]
    half = hidden // 2
    low, high = slice(0, half // 2), slice(half // 2, half)
    pair = pl.ds(0, 2)

    def device(x=x, zl=zl, zh=zh, y=y, core=core):
        return {"row": x * 2 + zl, "col": zh * 8 + y * 2 + core}

    to_core = device(core=other)
    to_next, to_prev = device(y=y_next), device(y=y_prev)
    to_zh, to_zl = device(zh=zo), device(zl=1 - zl)

    def along(d):
        return device(x=(x + d) % 4)

    pending = []
    slots = {}
    seen = set()

    def remote(name, j, src, dst, target):
        k = slots.setdefault((name, j), len(slots))
        return pltpu.make_async_remote_copy(
            src_ref=src, dst_ref=dst, send_sem=send_sem.at[k], recv_sem=recv_sem.at[k],
            device_id=target, device_id_type=MESH,
        )

    def send(name, j, src, dst, target):
        copy = remote(name, j, src, dst, target)
        copy.start()
        pending.append(copy)

    def arrive(name, j, dst):
        if (name, j) not in seen:
            seen.add((name, j))
            remote(name, j, dst, dst, to_core).wait_recv()

    stores = []

    def store(src, dst, sem):
        copy = pltpu.make_async_copy(src, dst, sem)
        copy.start()
        stores.append(copy)

    loads = [
        pltpu.make_async_copy(src, xo.at[0, i], load_sem.at[i])
        for i, src in enumerate((x_hbm, og_hbm))
    ]
    weights = [
        pltpu.make_async_copy(src, dst, weight_sem.at[i])
        for i, (src, dst) in enumerate(((wg_hbm, wg), (wu_hbm, wu), (wd_hbm, wd)))
    ]
    for copy in loads + weights:
        copy.start()

    barrier = pltpu.get_barrier_semaphore()
    peers = [to_core, to_next, to_prev, to_zh, to_zl] + [along(d) for d in (1, 2, 3)]
    for peer in peers:
        pl.semaphore_signal(barrier, inc=1, device_id=peer, device_id_type=MESH)
    pl.semaphore_wait(barrier, len(peers))

    def row_own(i):
        loads[i].wait()
        mine = xo.at[0, i]
        send(f"row{i}", PAIR, mine, xo.at[PAIR, i], to_zl)
        for d in (1, 3, 2):
            j = OFFSETS.index((d, 0))
            send(f"row{i}", j, mine, xo.at[j, i], along(4 - d))

    def row_pair(i):
        theirs = xo.at[PAIR, i]
        arrive(f"row{i}", PAIR, theirs)
        for d in (1, 3, 2):
            j = OFFSETS.index((d, 1))
            send(f"row{i}", j, theirs, xo.at[j, i], along(4 - d))

    def product(j, a, w, i, dims):
        if j == 0:
            weights[a].wait()
        else:
            arrive(f"row{i}", j, xo.at[j, i])
        left = xo[j, i]
        for c in range(2):
            cols = slice(c * half, (c + 1) * half)
            right = w[:, cols] if dims == NN else w[cols, :]
            part[j, c, :, :, a] = dot(left, right, dims).astype(BF16).reshape(4, 2, 16, half)
        send(f"core_in{a}", j, part.at[j, other, :, :, a], core_in.at[j, :, :, a], to_core)
        if a != 1 and j < LATE:
            store(xo.at[j, i], (xf_out, of_out)[i].at[j], store_sem.at[i, 0, j])

    def add(j, yy, zz, arrays):
        part[j, core, yy, zz, arrays] += core_in[j, yy, zz, arrays]

    def core_pair(j):
        for a in range(2):
            arrive(f"core_in{a}", j, core_in.at[j, :, :, a])
        both = slice(0, 2)
        add(j, y_far, 0, both)
        send("y1b+", j, part.at[j, core, y_far, 0, pair], y1b.at[j, 0], to_next)
        add(j, y_far, 1, both)
        send("y1b-", j, part.at[j, core, y_far, 1, pair], y1b.at[j, 1], to_prev)
        add(j, y_next, 1, both)
        send("y2b+e", j, part.at[j, core, y_next, 1, pair], y2b.at[j, 0, 1], to_next)
        add(j, y_prev, 0, both)
        send("y2b-e", j, part.at[j, core, y_prev, 0, pair], y2b.at[j, 1, 0], to_prev)
        add(j, y_next, 0, both)
        add(j, y_prev, 1, both)
        add(j, y, 0, both)
        add(j, y, 1, both)

    def first_next(j):
        arrive("y1b+", j, y1b.at[j, 0])
        part[j, core, y_next, 0, 0:2] += y1b[j, 0]
        send("y2b+l", j, part.at[j, core, y_next, 0, pair], y2b.at[j, 0, 0], to_next)

    def first_prev(j):
        arrive("y1b-", j, y1b.at[j, 1])
        part[j, core, y_prev, 1, 0:2] += y1b[j, 1]
        send("y2b-l", j, part.at[j, core, y_prev, 1, pair], y2b.at[j, 1, 1], to_prev)

    def second_pair(j):
        arrive("y2b+e", j, y2b.at[j, 0, 1])
        arrive("y2b+l", j, y2b.at[j, 0, 0])
        arrive("y2b-e", j, y2b.at[j, 1, 0])
        arrive("y2b-l", j, y2b.at[j, 1, 1])
        total = part[j, core, y, zo, 0:2].astype(F32) + y2b[j, 0, zo].astype(F32)
        part[j, core, y, zo, 0:2] = (total + y2b[j, 1, zo].astype(F32)).astype(BF16)
        send("zb", j, part.at[j, core, y, zo, pair], zb.at[j], to_zh)

    def core_last(j):
        arrive("core_in2", j, core_in.at[j, :, :, 2])
        for yy in range(4):
            add(j, yy, zo, 2)
        send("za", j, part.at[j, core, :, zo, 2], za.at[j], to_zh)
        for yy in range(4):
            add(j, yy, zh, 2)

    def first_last(j):
        arrive("za", j, za.at[j])
        part[j, core, y_far, zh, 2] += za[j, y_far]
        send("y1a+", j, part.at[j, core, y_far, zh, 2, :, low], y1a.at[j, 0], to_next)
        send("y1a-", j, part.at[j, core, y_far, zh, 2, :, high], y1a.at[j, 1], to_prev)
        part[j, core, y_next, zh, 2] += za[j, y_next]
        part[j, core, y_prev, zh, 2] += za[j, y_prev]

    def second_next(j):
        arrive("y1a+", j, y1a.at[j, 0])
        part[j, core, y_next, zh, 2, :, low] += y1a[j, 0]
        send("y2a+", j, part.at[j, core, y_next, zh, 2], y2a.at[j, 0], to_next)

    def second_prev(j):
        arrive("y1a-", j, y1a.at[j, 1])
        part[j, core, y_prev, zh, 2, :, high] += y1a[j, 1]
        send("y2a-", j, part.at[j, core, y_prev, zh, 2], y2a.at[j, 1], to_prev)

    def activations(j):
        arrive("y2a+", j, y2a.at[j, 0])
        arrive("y2a-", j, y2a.at[j, 1])
        arrive("zb", j, zb.at[j])
        for cols in (low, high):

            def term(*values):
                total = values[0].astype(F32)
                for value in values[1:]:
                    total = total + value.astype(F32)
                return total

            gate, up = (
                term(
                    part[j, core, y, zh, a, :, cols], y2b[j, 0, zh, a, :, cols],
                    y2b[j, 1, zh, a, :, cols], zb[j, a, :, cols],
                )
                for a in range(2)
            )
            act_grad = term(
                part[j, core, y, zh, 2, :, cols], za[j, y, :, cols],
                y2a[j, 0, :, cols], y2a[j, 1, :, cols],
            )
            act, slope = silu_parts(gate)
            full[j, core, y, zh, 0, :, cols] = (act_grad * up * slope).astype(BF16)
            full[j, core, y, zh, 1, :, cols] = (act_grad * act).astype(BF16)
            full[j, core, y, zh, 2, :, cols] = (act * up).astype(BF16)
        mine, single = full.at[j, core, y, zh, pair], full.at[j, core, y, zh, 2]
        send("gzb", j, mine, mine, to_zh)
        send("gya+", j, single, single, to_next)
        send("gya-", j, single, single, to_prev)
        send("gyb+o", j, mine, mine, to_next)
        send("gyb-o", j, mine, mine, to_prev)

    def spread_z(j):
        theirs = full.at[j, core, y, zo, pair]
        arrive("gzb", j, theirs)
        send("gyb+z", j, theirs, theirs, to_next)
        send("gyb-z", j, theirs, theirs, to_prev)

    def spread_single(j, name, yy, cols, target):
        piece = full.at[j, core, yy, zh, 2]
        arrive("gya" + name, j, piece)
        send("gfa" + name, j, piece.at[:, cols], piece.at[:, cols], target)

    def spread_pair(j, name, yy, z, target):
        arrive(f"gyb{name}o", j, full.at[j, core, yy, zh, pair])
        arrive(f"gyb{name}z", j, full.at[j, core, yy, zo, pair])
        piece = full.at[j, core, yy, z, pair]
        send("gfb" + name, j, piece, piece, target)

    def far_single(j):
        far = full.at[j, core, y_far, zh, 2]
        arrive("gfa+", j, far.at[:, low])
        arrive("gfa-", j, far.at[:, high])
        ring = full.at[j, core, :, zh, 2]
        send("gza", j, ring, ring, to_zh)

    def far_pair(j):
        arrive("gfb+", j, full.at[j, core, y_far, 0, pair])
        arrive("gfb-", j, full.at[j, core, y_far, 1, pair])
        whole = full.at[j, core, :, :, pair]
        send("gcb", j, whole, whole, to_core)

    def spread_rest(j):
        arrive("gza", j, full.at[j, core, :, zo, 2])
        whole = full.at[j, core, :, :, 2]
        send("gca", j, whole, whole, to_core)

    def send_mixed(j, i, value):
        mix[j, i] = value.astype(BF16)
        d = OFFSETS[j][0]
        if d:
            send(f"mix{i}", j, mix.at[j, i], mix_in.at[j, i], along(d))

    def acts(j, c, a):
        return full[j, c, :, :, a].reshape(rows, half)

    def store_acts(j, a, dst):
        if j < LATE:
            for c in range(2):
                store(
                    full.at[j, c, :, :, a], dst.at[j, :, :, :, pl.ds(c * half, half)],
                    store_sem.at[2 + a, c, j],
                )

    def output_mixed(j):
        arrive("gca", j, full.at[j, other, :, :, 2])
        value = dot(acts(j, 0, 2), wd[0:half, :], NN) + dot(acts(j, 1, 2), wd[half:hidden, :], NN)
        send_mixed(j, 0, value)
        store_acts(j, 2, h_out)

    def output_grad(j):
        arrive("gcb", j, full.at[j, other, :, :, pair])
        value = dot(acts(j, 0, 0), wg[:, 0:half], NT) + dot(acts(j, 1, 0), wg[:, half:hidden], NT)
        value = value + dot(acts(j, 0, 1), wu[:, 0:half], NT) + dot(acts(j, 1, 1), wu[:, half:hidden], NT)
        send_mixed(j, 1, value)
        store_acts(j, 0, gg_out)
        store_acts(j, 1, ug_out)

    def row_total(i, e):
        total = mix[OFFSETS.index((0, e)), i].astype(F32)
        for d in (1, 2, 3):
            j = OFFSETS.index((d, e))
            arrive(f"mix{i}", j, mix_in.at[j, i])
            total = total + mix_in[j, i].astype(F32)
        return total

    def row_sum(i):
        mix[PAIR, i] = row_total(i, 1).astype(BF16)
        send(f"mix_z{i}", 0, mix.at[PAIR, i], mix_z.at[i], to_zl)

    def finish(i):
        total = row_total(i, 0)
        arrive(f"mix_z{i}", 0, mix_z.at[i])
        outs[i] = (total + mix_z[i].astype(F32)).astype(BF16)
        store(outs.at[i], (mix_out, gi_out)[i], out_sem.at[i])

    done = []

    def weight_tile(k):
        tile = half // 2
        a, t = k // 4, k % 4
        units = full[LATE:, t // 2, :, :, a, :, (low, high)[t % 2]].reshape((CHUNKS - LATE) * rows, tile)
        side = xo[LATE:, a // 2].reshape((CHUNKS - LATE) * rows, width)
        if k >= 2:
            done[k - 2].wait()
        if a == 2:
            tall_tiles[k % 2] = dot(units, side, TN).astype(PARTIAL)
            src, dst = tall_tiles.at[k % 2], down_out.at[t]
        else:
            value = dot(side, units, TN).astype(PARTIAL)
            wide_tiles[k % 2] = value
            src, dst = wide_tiles.at[k % 2], (gate_out, up_out)[a].at[t]
        copy = pltpu.make_async_copy(src, dst, tile_sem.at[k])
        copy.start()
        done.append(copy)

    stages = {
        "R0": lambda j: row_own(0), "R1": lambda j: row_own(1),
        "P0": lambda j: row_pair(0), "P1": lambda j: row_pair(1),
        "G": lambda j: product(j, 0, wg, 0, NN),
        "U": lambda j: product(j, 1, wu, 0, NN),
        "A": lambda j: product(j, 2, wd, 1, NT),
        "CB": core_pair, "CA": core_last, "FB+": first_next, "FB-": first_prev, "FA": first_last,
        "SA+": second_next, "SA-": second_prev, "SB": second_pair, "ACT": activations, "ZB": spread_z,
        "YA+": lambda j: spread_single(j, "+", y_prev, low, to_next),
        "YA-": lambda j: spread_single(j, "-", y_next, high, to_prev),
        "YB+": lambda j: spread_pair(j, "+", y_prev, 0, to_next),
        "YB-": lambda j: spread_pair(j, "-", y_next, 1, to_prev),
        "ZF": far_single, "YF": far_pair, "ZA": spread_rest, "MIX": output_mixed, "GI": output_grad,
        "RS0": lambda j: row_sum(0), "RS1": lambda j: row_sum(1),
        "FI0": lambda j: finish(0), "FI1": lambda j: finish(1),
        "W": lambda j: weight_tile(len(done)),
    }
    for name, j in ORDER:
        stages[name](j)
    for copy in pending:
        copy.wait_send()
    for copy in stores + done[-2:]:
        copy.wait()


def exchange(inputs, gate_weight, up_weight, down_weight, out_grad):
    rows, width = inputs.shape
    hidden = gate_weight.shape[1]
    half = hidden // 2

    def buffer(*shape):
        return pltpu.VMEM(shape, BF16)

    def out(*shape, dtype=BF16):
        return jax.ShapeDtypeStruct(shape, dtype)

    wide = out(LATE, 4, 2, 16, hidden)
    thin = out(LATE, rows, width)
    own = out(rows, width)
    columns = out(4, width, hidden // 4, dtype=PARTIAL)
    any_space = pl.BlockSpec(memory_space=pl.ANY)
    outputs = (
        wide, wide, wide, thin, thin, own, own,
        columns, columns, out(4, hidden // 4, width, dtype=PARTIAL),
    )
    return pl.pallas_call(
        kernel,
        out_shape=outputs,
        in_specs=[any_space] * 5,
        out_specs=[any_space] * len(outputs),
        scratch_shapes=[
            buffer(CHUNKS, 2, rows, width),
            buffer(width, hidden),
            buffer(width, hidden),
            buffer(hidden, width),
            buffer(CHUNKS, 2, 4, 2, 3, 16, half),
            buffer(CHUNKS, 4, 2, 3, 16, half),
            buffer(CHUNKS, 2, 2, 16, half),
            buffer(CHUNKS, 2, 2, 2, 16, half),
            buffer(CHUNKS, 2, 16, half),
            buffer(CHUNKS, 4, 16, half),
            buffer(CHUNKS, 2, 16, half // 2),
            buffer(CHUNKS, 2, 16, half),
            buffer(CHUNKS, 2, 4, 2, 3, 16, half),
            buffer(CHUNKS, 2, rows, width),
            buffer(CHUNKS, 2, rows, width),
            buffer(2, rows, width),
            buffer(2, rows, width),
            pltpu.VMEM((2, width, hidden // 4), PARTIAL),
            pltpu.VMEM((2, hidden // 4, width), PARTIAL),
            pltpu.SemaphoreType.DMA((COPIES,)),
            pltpu.SemaphoreType.DMA((COPIES,)),
            pltpu.SemaphoreType.DMA((2,)),
            pltpu.SemaphoreType.DMA((3,)),
            pltpu.SemaphoreType.DMA((5, 2, LATE)),
            pltpu.SemaphoreType.DMA((12,)),
            pltpu.SemaphoreType.DMA((2,)),
        ],
        compiler_params=pltpu.CompilerParams(
            collective_id=0, has_side_effects=True, vmem_limit_bytes=62 << 20
        ),
    )(inputs, out_grad, gate_weight, up_weight, down_weight)


def weight_kernel(
    x_hbm, og_hbm, gg_hbm, ug_hbm, h_hbm, gate_hbm, up_hbm, down_hbm, mix_hbm, gi_hbm,
    mix_out, gi_out, gate_out, up_out, down_out,
    x, og, acts, parts, wide, tall, own, left_sem, part_sem, out_sem, own_sem,
):
    tiles, tile = wide.shape[1], wide.shape[3]
    pieces = ((x_hbm, x), (og_hbm, og), (gg_hbm, acts.at[0]), (ug_hbm, acts.at[1]), (h_hbm, acts.at[2]))
    loads = [pltpu.make_async_copy(src, dst, left_sem.at[i]) for i, (src, dst) in enumerate(pieces)]
    mine = [pltpu.make_async_copy(src, own.at[i], own_sem.at[i]) for i, src in enumerate((mix_hbm, gi_hbm))]
    sums = [
        [pltpu.make_async_copy(src.at[t], parts.at[a, t], part_sem.at[a, t]) for t in range(tiles)]
        for a, src in enumerate((gate_hbm, up_hbm, down_hbm))
    ]
    order = ((0, (0, 2)), (1, (3,)), (2, (1, 4)))
    for a, needs in order:
        for i in needs:
            loads[i].start()
        for copy in sums[a]:
            copy.start()
    for copy in mine:
        copy.start()
    stores = []
    for a, needs in order:
        for i in needs:
            loads[i].wait()
        for t in range(tiles):
            cols = slice(t * tile, (t + 1) * tile)
            sums[a][t].wait()
            if a == 2:
                tall[cols, :] = parts[a, t].astype(F32) + dot(acts[2, :, cols], og[...], TN)
                src, dst = tall.at[pl.ds(t * tile, tile)], down_out.at[pl.ds(t * tile, tile)]
            else:
                wide[a, t] = parts[a, t].astype(F32) + dot(x[...], acts[a, :, cols], TN)
                src, dst = wide.at[a, t], (gate_out, up_out)[a].at[:, pl.ds(t * tile, tile)]
            stores.append(pltpu.make_async_copy(src, dst, out_sem.at[a, t]))
            stores[-1].start()
    for i, copy in enumerate(mine):
        copy.wait()
        stores.append(pltpu.make_async_copy(own.at[i], (mix_out, gi_out)[i], own_sem.at[2 + i]))
        stores[-1].start()
    for copy in stores:
        copy.wait()


def weight_grads(x, og, gg, ug, h, gate_part, up_part, down_part, mixed, grad_input):
    tokens, width = x.shape
    hidden = h.shape[1]
    tiles = gate_part.shape[0]
    tile = hidden // tiles
    any_space = pl.BlockSpec(memory_space=pl.ANY)
    return pl.pallas_call(
        weight_kernel,
        out_shape=(
            jax.ShapeDtypeStruct(mixed.shape, BF16),
            jax.ShapeDtypeStruct(mixed.shape, BF16),
            jax.ShapeDtypeStruct((width, hidden), F32),
            jax.ShapeDtypeStruct((width, hidden), F32),
            jax.ShapeDtypeStruct((hidden, width), F32),
        ),
        in_specs=[any_space] * 10,
        out_specs=[any_space] * 5,
        scratch_shapes=[
            pltpu.VMEM((tokens, width), BF16),
            pltpu.VMEM((tokens, width), BF16),
            pltpu.VMEM((3, tokens, hidden), BF16),
            pltpu.VMEM((3, tiles, width, tile), PARTIAL),
            pltpu.VMEM((2, tiles, width, tile), F32),
            pltpu.VMEM((hidden, width), F32),
            pltpu.VMEM((2,) + mixed.shape, BF16),
            pltpu.SemaphoreType.DMA((5,)),
            pltpu.SemaphoreType.DMA((3, tiles)),
            pltpu.SemaphoreType.DMA((3, tiles)),
            pltpu.SemaphoreType.DMA((4,)),
        ],
        compiler_params=pltpu.CompilerParams(vmem_limit_bytes=62 << 20),
    )(x, og, gg, ug, h, gate_part, up_part, down_part, mixed, grad_input)


def body(inputs, gate_weight, up_weight, down_weight, out_grad):
    h, gg, ug, x, og, mixed, grad_input, gate_part, up_part, down_part = exchange(
        inputs, gate_weight, up_weight, down_weight, out_grad
    )
    width = inputs.shape[1]
    hidden = gate_weight.shape[1]
    return weight_grads(
        x.reshape(-1, width), og.reshape(-1, width),
        gg.reshape(-1, hidden), ug.reshape(-1, hidden), h.reshape(-1, hidden),
        gate_part, up_part, down_part, mixed, grad_input,
    )


def solution(mesh):
    in_specs = (P("row", "col"), P("col", "row"), P("col", "row"), P("row", "col"), P("row", "col"))
    out_specs = (
        P("row", "col"),
        P("row", "col"),
        P("col", "row"),
        P("col", "row"),
        P("row", "col"),
    )
    return jax.shard_map(body, mesh=mesh, in_specs=in_specs, out_specs=out_specs, check_vma=False)
```

```python
import functools

import jax
import jax.numpy as jnp
from jax import lax
from jax.experimental import pallas as pl
from jax.experimental.pallas import tpu as pltpu
from jax.sharding import PartitionSpec as P

MESH = pl.DeviceIdType.MESH
BF16, F32 = jnp.bfloat16, jnp.float32
PARTIAL = BF16
OFFSETS = ((0, 0), (0, 1), (2, 1), (1, 1), (3, 1), (2, 0), (1, 0), (3, 0))
CHUNKS = len(OFFSETS)
PAIR = OFFSETS.index((0, 1))
LATE = 2
DIRECT = ()
COPIES = 270
VMEM_LIMIT = 62 << 20
NN = (((1,), (0,)), ((), ()))
TN = (((0,), (0,)), ((), ()))


def dot(left, right, dims):
    return lax.dot_general(left, right, dims, preferred_element_type=F32)


def silu_parts(gate):
    sig = jax.nn.sigmoid(gate)
    return gate * sig, sig * (1.0 + gate * (1.0 - sig))


ORDER = (
    ("R0", 0), ("G", 0), ("U", 0), ("R1", 0), ("A", 0), ("CB", 0), ("CA", 0), ("G", 6), ("P0", 0), ("G", 1),
    ("U", 1), ("FB+", 0), ("FB-", 0), ("U", 6), ("G", 7), ("CB", 1), ("G", 5), ("T0", 0), ("CB", 6), ("A", 1),
    ("SB", 0), ("FA", 0), ("P1", 0), ("U", 5), ("CA", 1), ("FB-", 1), ("U", 7), ("T1", 0), ("CB", 5), ("A", 5),
    ("FB+", 6), ("FB-", 6), ("CB", 7), ("FB+", 1), ("G", 4), ("SA+", 0), ("CA", 5), ("U", 4), ("G", 3), ("FA", 1),
    ("FB+", 5), ("U", 3), ("CB", 4), ("FB-", 5), ("A", 7), ("CB", 3), ("SA-", 0), ("A", 6), ("A", 4), ("CA", 7),
    ("A", 3), ("FB+", 7), ("CA", 6), ("CA", 4), ("SB", 6), ("FA", 5), ("CA", 3), ("G", 2), ("U", 2), ("SA-", 1),
    ("A", 2), ("SA+", 1), ("SB", 1), ("FB-", 4), ("CB", 2), ("FB-", 7), ("FA", 7), ("CA", 2), ("FB+", 4), ("SB", 5),
    ("FA", 6), ("FB-", 3), ("FB+", 3), ("SA-", 5), ("FA", 4), ("SA+", 5), ("FB-", 2), ("FB+", 2), ("FA", 3),
    ("SA+", 7), ("SB", 7), ("SA-", 7), ("SB", 4), ("SA-", 6), ("SA+", 6), ("SB", 3), ("SA+", 4), ("FA", 2),
    ("SA-", 4), ("ACT", 5), ("SB", 2), ("SA+", 3), ("SA-", 3), ("SA-", 2), ("ACT", 4), ("YA+", 5), ("SA+", 2),
    ("YA-", 5), ("ACT", 3), ("YA+", 4), ("YA-", 4), ("ZB", 4), ("ZF", 5), ("ACT", 2), ("YA-", 3), ("YA+", 3),
    ("ZB", 3), ("ZF", 4), ("YB-", 4), ("YB+", 4), ("ACT", 1), ("YA-", 2), ("YA+", 2), ("ZA", 5), ("ZF", 3),
    ("ZB", 2), ("MIX", 5), ("YB+", 3), ("YB-", 3), ("ACT", 7), ("YF", 4), ("YA-", 1), ("ZA", 4), ("YA+", 1),
    ("GI", 4), ("ZF", 2), ("MIX", 4), ("YB-", 2), ("YB+", 2), ("ACT", 6), ("ZA", 3), ("YF", 3), ("YA-", 7),
    ("YA+", 7), ("ZB", 7), ("MIX", 3), ("GI", 3), ("ZF", 1), ("ZA", 2), ("YF", 2), ("ZB", 5), ("YA-", 6),
    ("YA+", 6), ("ZB", 6), ("MIX", 2), ("GI", 2), ("ZF", 7), ("YB-", 7), ("YB+", 7), ("ZA", 1), ("YB-", 5),
    ("YB+", 5), ("ACT", 0), ("ZF", 6), ("MIX", 1), ("YB-", 6), ("YB+", 6), ("YF", 7), ("ZA", 7), ("RS0", 0),
    ("YF", 5), ("ZB", 1), ("GI", 7), ("MIX", 7), ("YA-", 0), ("YA+", 0), ("GI", 5), ("ZA", 6), ("YF", 6), ("ZB", 0),
    ("MIX", 6), ("YB-", 1), ("YB+", 1), ("GI", 6), ("ZF", 0), ("W", 0), ("YB+", 0), ("W", 0), ("YB-", 0), ("W", 0),
    ("W", 0), ("YF", 1), ("W", 0), ("W", 0), ("W", 0), ("GI", 1), ("ZA", 0), ("RS1", 0), ("YF", 0), ("W", 0),
    ("MIX", 0), ("FI0", 0), ("GI", 0), ("W", 0), ("W", 0), ("W", 0), ("FI1", 0), ("W", 0),
)


def kernel(
    x_hbm, og_hbm, wg_hbm, wu_hbm, wd_hbm,
    h_out, gg_out, ug_out, xf_out, of_out, mix_out, gi_out, gate_out, up_out, down_out,
    xo, wg, wu, wd, wgt, wut, wdt, part, core_in, y1b, y2b, zb, za, y1a, y2a, full, mix, mix_in, mix_z, outs, tiles,
    send_sem, recv_sem, load_sem, weight_sem, store_sem, tile_sem, out_sem,
):
    row, col = lax.axis_index("row"), lax.axis_index("col")
    x, zl = row // 2, row % 2
    zh, y, core = col // 8, (col // 2) % 4, col % 2
    zo, other = 1 - zh, 1 - core
    y_next, y_prev, y_far = (y + 1) % 4, (y + 3) % 4, (y + 2) % 4
    rows, width = x_hbm.shape
    hidden = wg_hbm.shape[1]
    half = hidden // 2
    low, high = slice(0, half // 2), slice(half // 2, half)
    pair = pl.ds(0, 2)

    def device(x=x, zl=zl, zh=zh, y=y, core=core):
        return {"row": x * 2 + zl, "col": zh * 8 + y * 2 + core}

    to_core = device(core=other)
    to_next, to_prev = device(y=y_next), device(y=y_prev)
    to_zh, to_zl = device(zh=zo), device(zl=1 - zl)

    def along(d):
        return device(x=(x + d) % 4)

    pending = []
    slots = {}
    seen = set()

    def remote(name, j, src, dst, target):
        k = slots.setdefault((name, j), len(slots))
        return pltpu.make_async_remote_copy(
            src_ref=src, dst_ref=dst, send_sem=send_sem.at[k], recv_sem=recv_sem.at[k],
            device_id=target, device_id_type=MESH,
        )

    def send(name, j, src, dst, target):
        copy = remote(name, j, src, dst, target)
        copy.start()
        pending.append(copy)

    def arrive(name, j, dst):
        if (name, j) not in seen:
            seen.add((name, j))
            remote(name, j, dst, dst, to_core).wait_recv()

    settled = []

    def settle(count):
        while len(settled) < count:
            copy = pending[len(settled)]
            copy.wait_send()
            settled.append(copy)

    stores = []

    def store(src, dst, sem):
        copy = pltpu.make_async_copy(src, dst, sem)
        copy.start()
        stores.append(copy)

    loads = [
        pltpu.make_async_copy(src, xo.at[0, i], load_sem.at[i])
        for i, src in enumerate((x_hbm, og_hbm))
    ]
    weights = [
        pltpu.make_async_copy(src, dst, weight_sem.at[i])
        for i, (src, dst) in enumerate(((wg_hbm, wg), (wu_hbm, wu), (wd_hbm, wd)))
    ]
    for copy in loads + weights:
        copy.start()

    barrier = pltpu.get_barrier_semaphore()
    to_next_zh, to_prev_zh = device(zh=zo, y=y_next), device(zh=zo, y=y_prev)
    peers = [to_core, to_next, to_prev, to_zh, to_zl, to_next_zh, to_prev_zh] + [along(d) for d in (1, 2, 3)]
    for peer in peers:
        pl.semaphore_signal(barrier, inc=1, device_id=peer, device_id_type=MESH)
    pl.semaphore_wait(barrier, len(peers))

    def row_own(i):
        loads[i].wait()
        mine = xo.at[0, i]
        send(f"row{i}", PAIR, mine, xo.at[PAIR, i], to_zl)
        for d in (1, 3, 2):
            j = OFFSETS.index((d, 0))
            send(f"row{i}", j, mine, xo.at[j, i], along(4 - d))

    def row_pair(i):
        theirs = xo.at[PAIR, i]
        arrive(f"row{i}", PAIR, theirs)
        for d in (1, 3, 2):
            j = OFFSETS.index((d, 1))
            send(f"row{i}", j, theirs, xo.at[j, i], along(4 - d))

    def transpose(src, dst):
        across = src.shape[0] < src.shape[1]
        size = max(src.shape) // 8
        for k in range(8):
            block = slice(k * size, (k + 1) * size)
            if across:
                dst[block, :] = src[:, block].T
            else:
                dst[:, block] = src[block, :].T

    def send_product(j, a):
        send(f"core_in{a}", j, part.at[j, other, :, :, a], core_in.at[j, :, :, a], to_core)

    def product(j, a, w, i):
        if j == 0:
            weights[a].wait()
            if a == 2:
                transpose(wd, wdt)
        else:
            arrive(f"row{i}", j, xo.at[j, i])
        left = xo[j, i]
        for c in range(2):
            cols = slice(c * half, (c + 1) * half)
            part[j, c, :, :, a] = dot(left, w[:, cols], NN).astype(BF16).reshape(4, 2, 16, half)
        send_product(j, a)
        if a != 1 and j < LATE:
            store(xo.at[j, i], (xf_out, of_out)[i].at[j], store_sem.at[i, 0, j])

    def add(j, yy, zz, arrays):
        part[j, core, yy, zz, arrays] += core_in[j, yy, zz, arrays]

    def core_pair(j):
        for a in range(2):
            arrive(f"core_in{a}", j, core_in.at[j, :, :, a])
        both = slice(0, 2)
        add(j, y_far, 0, both)
        send("y1b+", j, part.at[j, core, y_far, 0, pair], y1b.at[j, 0], to_next)
        add(j, y_far, 1, both)
        send("y1b-", j, part.at[j, core, y_far, 1, pair], y1b.at[j, 1], to_prev)
        add(j, y_next, 1, both)
        send("y2b+e", j, part.at[j, core, y_next, 1, pair], y2b.at[j, 0, 1], to_next)
        add(j, y_prev, 0, both)
        send("y2b-e", j, part.at[j, core, y_prev, 0, pair], y2b.at[j, 1, 0], to_prev)
        add(j, y_next, 0, both)
        add(j, y_prev, 1, both)
        add(j, y, 0, both)
        add(j, y, 1, both)

    def first_next(j):
        arrive("y1b+", j, y1b.at[j, 0])
        part[j, core, y_next, 0, 0:2] += y1b[j, 0]
        send("y2b+l", j, part.at[j, core, y_next, 0, pair], y2b.at[j, 0, 0], to_next)

    def first_prev(j):
        arrive("y1b-", j, y1b.at[j, 1])
        part[j, core, y_prev, 1, 0:2] += y1b[j, 1]
        send("y2b-l", j, part.at[j, core, y_prev, 1, pair], y2b.at[j, 1, 1], to_prev)

    def second_pair(j):
        arrive("y2b+e", j, y2b.at[j, 0, 1])
        arrive("y2b+l", j, y2b.at[j, 0, 0])
        arrive("y2b-e", j, y2b.at[j, 1, 0])
        arrive("y2b-l", j, y2b.at[j, 1, 1])
        total = part[j, core, y, zo, 0:2].astype(F32) + y2b[j, 0, zo].astype(F32)
        part[j, core, y, zo, 0:2] = (total + y2b[j, 1, zo].astype(F32)).astype(BF16)
        send("zb", j, part.at[j, core, y, zo, pair], zb.at[j], to_zh)

    def core_last(j):
        arrive("core_in2", j, core_in.at[j, :, :, 2])
        for yy in range(4):
            add(j, yy, zo, 2)
        send("za", j, part.at[j, core, :, zo, 2], za.at[j], to_zh)
        for yy in range(4):
            add(j, yy, zh, 2)

    def first_last(j):
        arrive("za", j, za.at[j])
        part[j, core, y_far, zh, 2] += za[j, y_far]
        send("y1a+", j, part.at[j, core, y_far, zh, 2, :, low], y1a.at[j, 0], to_next)
        send("y1a-", j, part.at[j, core, y_far, zh, 2, :, high], y1a.at[j, 1], to_prev)
        part[j, core, y_next, zh, 2] += za[j, y_next]
        part[j, core, y_prev, zh, 2] += za[j, y_prev]

    def second_next(j):
        arrive("y1a+", j, y1a.at[j, 0])
        part[j, core, y_next, zh, 2, :, low] += y1a[j, 0]
        send("y2a+", j, part.at[j, core, y_next, zh, 2], y2a.at[j, 0], to_next)

    def second_prev(j):
        arrive("y1a-", j, y1a.at[j, 1])
        part[j, core, y_prev, zh, 2, :, high] += y1a[j, 1]
        send("y2a-", j, part.at[j, core, y_prev, zh, 2], y2a.at[j, 1], to_prev)

    def activations(j):
        arrive("y2a+", j, y2a.at[j, 0])
        arrive("y2a-", j, y2a.at[j, 1])
        arrive("zb", j, zb.at[j])
        for cols in (low, high):

            def term(*values):
                total = values[0].astype(F32)
                for value in values[1:]:
                    total = total + value.astype(F32)
                return total

            gate, up = (
                term(
                    part[j, core, y, zh, a, :, cols], y2b[j, 0, zh, a, :, cols],
                    y2b[j, 1, zh, a, :, cols], zb[j, a, :, cols],
                )
                for a in range(2)
            )
            act_grad = term(
                part[j, core, y, zh, 2, :, cols], za[j, y, :, cols],
                y2a[j, 0, :, cols], y2a[j, 1, :, cols],
            )
            act, slope = silu_parts(gate)
            full[j, core, y, zh, 0, :, cols] = (act_grad * up * slope).astype(BF16)
            full[j, core, y, zh, 1, :, cols] = (act_grad * act).astype(BF16)
            full[j, core, y, zh, 2, :, cols] = (act * up).astype(BF16)
        mine, single = full.at[j, core, y, zh, pair], full.at[j, core, y, zh, 2]
        send("gzb", j, mine, mine, to_zh)
        send("gya+", j, single, single, to_next)
        send("gya-", j, single, single, to_prev)
        send("gyb+o", j, mine, mine, to_next)
        send("gyb-o", j, mine, mine, to_prev)
        if j in DIRECT:
            send("gyb+z", j, mine, mine, to_next_zh)
            send("gyb-z", j, mine, mine, to_prev_zh)
            send("gza_o", j, single, single, to_zh)

    def spread_z(j):
        theirs = full.at[j, core, y, zo, pair]
        arrive("gzb", j, theirs)
        if j not in DIRECT:
            send("gyb+z", j, theirs, theirs, to_next)
            send("gyb-z", j, theirs, theirs, to_prev)

    def spread_single(j, name, yy, cols, target):
        piece = full.at[j, core, yy, zh, 2]
        arrive("gya" + name, j, piece)
        send("gfa" + name, j, piece.at[:, cols], piece.at[:, cols], target)
        if j in DIRECT:
            send("gza" + name, j, piece, piece, to_zh)

    def spread_pair(j, name, yy, z, target):
        arrive(f"gyb{name}o", j, full.at[j, core, yy, zh, pair])
        arrive(f"gyb{name}z", j, full.at[j, core, yy, zo, pair])
        piece = full.at[j, core, yy, z, pair]
        send("gfb" + name, j, piece, piece, target)

    def far_single(j):
        far = full.at[j, core, y_far, zh, 2]
        arrive("gfa+", j, far.at[:, low])
        arrive("gfa-", j, far.at[:, high])
        if j in DIRECT:
            send("gza_f", j, far, far, to_zh)
        else:
            ring = full.at[j, core, :, zh, 2]
            send("gza", j, ring, ring, to_zh)

    def far_pair(j):
        arrive("gfb+", j, full.at[j, core, y_far, 0, pair])
        arrive("gfb-", j, full.at[j, core, y_far, 1, pair])
        whole = full.at[j, core, :, :, pair]
        send("gcb", j, whole, whole, to_core)

    def spread_rest(j):
        if j in DIRECT:
            for name, yy in (("gza_o", y), ("gza+", y_prev), ("gza-", y_next), ("gza_f", y_far)):
                arrive(name, j, full.at[j, core, yy, zo, 2])
        else:
            arrive("gza", j, full.at[j, core, :, zo, 2])
        whole = full.at[j, core, :, :, 2]
        send("gca", j, whole, whole, to_core)

    def send_mixed(j, i, value):
        mix[j, i] = value.astype(BF16)
        d = OFFSETS[j][0]
        if d:
            send(f"mix{i}", j, mix.at[j, i], mix_in.at[j - 2, i], along(d))

    def acts(j, c, a):
        return full[j, c, :, :, a].reshape(rows, half)

    def store_acts(j, a, dst):
        if j < LATE:
            for c in range(2):
                store(
                    full.at[j, c, :, :, a], dst.at[j, :, :, :, pl.ds(c * half, half)],
                    store_sem.at[2 + a, c, j],
                )

    def output_mixed(j):
        arrive("gca", j, full.at[j, other, :, :, 2])
        value = dot(acts(j, 0, 2), wd[0:half, :], NN) + dot(acts(j, 1, 2), wd[half:hidden, :], NN)
        send_mixed(j, 0, value)
        store_acts(j, 2, h_out)

    def output_grad(j):
        arrive("gcb", j, full.at[j, other, :, :, pair])
        value = dot(acts(j, 0, 0), wgt[0:half, :], NN) + dot(acts(j, 1, 0), wgt[half:hidden, :], NN)
        value = value + dot(acts(j, 0, 1), wut[0:half, :], NN) + dot(acts(j, 1, 1), wut[half:hidden, :], NN)
        send_mixed(j, 1, value)
        store_acts(j, 0, gg_out)
        store_acts(j, 1, ug_out)

    def row_total(i, e):
        total = mix[OFFSETS.index((0, e)), i].astype(F32)
        for d in (1, 2, 3):
            j = OFFSETS.index((d, e))
            arrive(f"mix{i}", j, mix_in.at[j - 2, i])
            total = total + mix_in[j - 2, i].astype(F32)
        return total

    def row_sum(i):
        mix[PAIR, i] = row_total(i, 1).astype(BF16)
        send(f"mix_z{i}", 0, mix.at[PAIR, i], mix_z.at[i], to_zl)

    def finish(i):
        total = row_total(i, 0)
        arrive(f"mix_z{i}", 0, mix_z.at[i])
        outs[i] = (total + mix_z[i].astype(F32)).astype(BF16)
        store(outs.at[i], (mix_out, gi_out)[i], out_sem.at[i])

    done = []

    def weight_tile(k):
        tile = half // 2
        a, t = k // 4, k % 4
        units = full[LATE:, t // 2, :, :, a, :, (low, high)[t % 2]].reshape((CHUNKS - LATE) * rows, tile)
        side = xo[LATE:, a // 2].reshape((CHUNKS - LATE) * rows, width)
        if k >= 2:
            done[k - 2].wait()
        if a == 2:
            tiles[k % 2] = dot(units, side, TN).astype(PARTIAL)
            dst = down_out.at[t]
        else:
            tiles[k % 2] = dot(side, units, TN).astype(PARTIAL)
            dst = (gate_out, up_out)[a].at[t]
        copy = pltpu.make_async_copy(tiles.at[k % 2], dst, tile_sem.at[k])
        copy.start()
        done.append(copy)

    stages = {
        "R0": lambda j: row_own(0), "R1": lambda j: row_own(1),
        "P0": lambda j: row_pair(0), "P1": lambda j: row_pair(1),
        "G": lambda j: product(j, 0, wg, 0),
        "U": lambda j: product(j, 1, wu, 0),
        "A": lambda j: product(j, 2, wdt, 1),
        "T0": lambda j: transpose(wg, wgt), "T1": lambda j: transpose(wu, wut),
        "CB": core_pair, "CA": core_last, "FB+": first_next, "FB-": first_prev, "FA": first_last,
        "SA+": second_next, "SA-": second_prev, "SB": second_pair, "ACT": activations, "ZB": spread_z,
        "YA+": lambda j: spread_single(j, "+", y_prev, low, to_next),
        "YA-": lambda j: spread_single(j, "-", y_next, high, to_prev),
        "YB+": lambda j: spread_pair(j, "+", y_prev, 0, to_next),
        "YB-": lambda j: spread_pair(j, "-", y_next, 1, to_prev),
        "ZF": far_single, "YF": far_pair, "ZA": spread_rest, "MIX": output_mixed, "GI": output_grad,
        "RS0": lambda j: row_sum(0), "RS1": lambda j: row_sum(1),
        "FI0": lambda j: finish(0), "FI1": lambda j: finish(1),
        "W": lambda j: weight_tile(len(done)),
    }
    sent = []
    for name, j in ORDER:
        stages[name](j)
        sent.append(len(pending))
        if len(sent) > 40:
            settle(sent[-41])
    settle(len(pending))
    for copy in stores + done[-2:]:
        copy.wait()


def exchange(inputs, gate_weight, up_weight, down_weight, out_grad):
    rows, width = inputs.shape
    hidden = gate_weight.shape[1]
    half = hidden // 2

    def buffer(*shape):
        return pltpu.VMEM(shape, BF16)

    def out(*shape, dtype=BF16):
        return jax.ShapeDtypeStruct(shape, dtype)

    wide = out(LATE, 4, 2, 16, hidden)
    thin = out(LATE, rows, width)
    own = out(rows, width)
    columns = out(4, width, hidden // 4, dtype=PARTIAL)
    any_space = pl.BlockSpec(memory_space=pl.ANY)
    outputs = (
        wide, wide, wide, thin, thin, own, own,
        columns, columns, out(4, hidden // 4, width, dtype=PARTIAL),
    )
    return pl.pallas_call(
        kernel,
        out_shape=outputs,
        in_specs=[any_space] * 5,
        out_specs=[any_space] * len(outputs),
        scratch_shapes=[
            buffer(CHUNKS, 2, rows, width),
            buffer(width, hidden),
            buffer(width, hidden),
            buffer(hidden, width),
            buffer(hidden, width),
            buffer(hidden, width),
            buffer(width, hidden),
            buffer(CHUNKS, 2, 4, 2, 3, 16, half),
            buffer(CHUNKS, 4, 2, 3, 16, half),
            buffer(CHUNKS, 2, 2, 16, half),
            buffer(CHUNKS, 2, 2, 2, 16, half),
            buffer(CHUNKS, 2, 16, half),
            buffer(CHUNKS, 4, 16, half),
            buffer(CHUNKS, 2, 16, half // 2),
            buffer(CHUNKS, 2, 16, half),
            buffer(CHUNKS, 2, 4, 2, 3, 16, half),
            buffer(CHUNKS, 2, rows, width),
            buffer(CHUNKS - 2, 2, rows, width),
            buffer(2, rows, width),
            buffer(2, rows, width),
            pltpu.VMEM((2, width, hidden // 4), PARTIAL),
            pltpu.SemaphoreType.DMA((COPIES,)),
            pltpu.SemaphoreType.DMA((COPIES,)),
            pltpu.SemaphoreType.DMA((2,)),
            pltpu.SemaphoreType.DMA((3,)),
            pltpu.SemaphoreType.DMA((5, 2, LATE)),
            pltpu.SemaphoreType.DMA((12,)),
            pltpu.SemaphoreType.DMA((2,)),
        ],
        compiler_params=pltpu.CompilerParams(
            collective_id=0, has_side_effects=True, vmem_limit_bytes=VMEM_LIMIT
        ),
    )(inputs, out_grad, gate_weight, up_weight, down_weight)


def weight_kernel(
    x_hbm, og_hbm, gg_hbm, ug_hbm, h_hbm, gate_hbm, up_hbm, down_hbm, mix_hbm, gi_hbm,
    mix_out, gi_out, gate_out, up_out, down_out,
    x, og, acts, parts, wide, tall, own, left_sem, part_sem, out_sem, own_sem,
):
    tiles, tile = wide.shape[1], wide.shape[3]
    pieces = ((x_hbm, x), (og_hbm, og), (gg_hbm, acts.at[0]), (ug_hbm, acts.at[1]), (h_hbm, acts.at[2]))
    loads = [pltpu.make_async_copy(src, dst, left_sem.at[i]) for i, (src, dst) in enumerate(pieces)]
    mine = [pltpu.make_async_copy(src, own.at[i], own_sem.at[i]) for i, src in enumerate((mix_hbm, gi_hbm))]
    sums = [
        [pltpu.make_async_copy(src.at[t], parts.at[a, t], part_sem.at[a, t]) for t in range(tiles)]
        for a, src in enumerate((gate_hbm, up_hbm, down_hbm))
    ]
    order = ((0, (0, 2)), (1, (3,)), (2, (1, 4)))
    for a, needs in order:
        for i in needs:
            loads[i].start()
        for copy in sums[a]:
            copy.start()
    for copy in mine:
        copy.start()
    stores = []
    for a, needs in order:
        for i in needs:
            loads[i].wait()
        for t in range(tiles):
            cols = slice(t * tile, (t + 1) * tile)
            sums[a][t].wait()
            if a == 2:
                tall[cols, :] = parts[a, t].astype(F32) + dot(acts[2, :, cols], og[...], TN)
                src, dst = tall.at[pl.ds(t * tile, tile)], down_out.at[pl.ds(t * tile, tile)]
            else:
                wide[a, t] = parts[a, t].astype(F32) + dot(x[...], acts[a, :, cols], TN)
                src, dst = wide.at[a, t], (gate_out, up_out)[a].at[:, pl.ds(t * tile, tile)]
            stores.append(pltpu.make_async_copy(src, dst, out_sem.at[a, t]))
            stores[-1].start()
    for i, copy in enumerate(mine):
        copy.wait()
        stores.append(pltpu.make_async_copy(own.at[i], (mix_out, gi_out)[i], own_sem.at[2 + i]))
        stores[-1].start()
    for copy in stores:
        copy.wait()


def weight_grads(x, og, gg, ug, h, gate_part, up_part, down_part, mixed, grad_input):
    tokens, width = x.shape
    hidden = h.shape[1]
    tiles = gate_part.shape[0]
    tile = hidden // tiles
    any_space = pl.BlockSpec(memory_space=pl.ANY)
    return pl.pallas_call(
        weight_kernel,
        out_shape=(
            jax.ShapeDtypeStruct(mixed.shape, BF16),
            jax.ShapeDtypeStruct(mixed.shape, BF16),
            jax.ShapeDtypeStruct((width, hidden), F32),
            jax.ShapeDtypeStruct((width, hidden), F32),
            jax.ShapeDtypeStruct((hidden, width), F32),
        ),
        in_specs=[any_space] * 10,
        out_specs=[any_space] * 5,
        scratch_shapes=[
            pltpu.VMEM((tokens, width), BF16),
            pltpu.VMEM((tokens, width), BF16),
            pltpu.VMEM((3, tokens, hidden), BF16),
            pltpu.VMEM((3, tiles, width, tile), PARTIAL),
            pltpu.VMEM((2, tiles, width, tile), F32),
            pltpu.VMEM((hidden, width), F32),
            pltpu.VMEM((2,) + mixed.shape, BF16),
            pltpu.SemaphoreType.DMA((5,)),
            pltpu.SemaphoreType.DMA((3, tiles)),
            pltpu.SemaphoreType.DMA((3, tiles)),
            pltpu.SemaphoreType.DMA((4,)),
        ],
        compiler_params=pltpu.CompilerParams(vmem_limit_bytes=VMEM_LIMIT),
    )(x, og, gg, ug, h, gate_part, up_part, down_part, mixed, grad_input)


def body(inputs, gate_weight, up_weight, down_weight, out_grad):
    h, gg, ug, x, og, mixed, grad_input, gate_part, up_part, down_part = exchange(
        inputs, gate_weight, up_weight, down_weight, out_grad
    )
    width = inputs.shape[1]
    hidden = gate_weight.shape[1]
    return weight_grads(
        x.reshape(-1, width), og.reshape(-1, width),
        gg.reshape(-1, hidden), ug.reshape(-1, hidden), h.reshape(-1, hidden),
        gate_part, up_part, down_part, mixed, grad_input,
    )


def solution(mesh):
    in_specs = (P("row", "col"), P("col", "row"), P("col", "row"), P("row", "col"), P("row", "col"))
    out_specs = (
        P("row", "col"),
        P("row", "col"),
        P("col", "row"),
        P("col", "row"),
        P("row", "col"),
    )
    return jax.shard_map(body, mesh=mesh, in_specs=in_specs, out_specs=out_specs, check_vma=False)
```

```python
import functools

import jax
import jax.numpy as jnp
from jax import lax
from jax.experimental import pallas as pl
from jax.experimental.pallas import tpu as pltpu
from jax.sharding import PartitionSpec as P

MESH = pl.DeviceIdType.MESH
BF16, F32 = jnp.bfloat16, jnp.float32
PARTIAL = BF16
OFFSETS = ((0, 0), (0, 1), (2, 1), (1, 1), (3, 1), (2, 0), (1, 0), (3, 0))
CHUNKS = len(OFFSETS)
PAIR = OFFSETS.index((0, 1))
LATE = 2
SPLIT = 5
DIRECT = ()
COPIES = 270
VMEM_LIMIT = 62 << 20
NN = (((1,), (0,)), ((), ()))
TN = (((0,), (0,)), ((), ()))


def dot(left, right, dims):
    return lax.dot_general(left, right, dims, preferred_element_type=F32)


def silu_parts(gate):
    sig = jax.nn.sigmoid(gate)
    return gate * sig, sig * (1.0 + gate * (1.0 - sig))


ORDER = (
    ("R0", 0), ("R1", 0), ("G", 0), ("U", 0), ("A", 0), ("CB", 0), ("CA", 0), ("G", 1), ("U", 1), ("G", 7),
    ("P0", 0), ("FB+", 0), ("FB-", 0), ("U", 7), ("CB", 1), ("T1", 0), ("G", 5), ("CB", 7), ("A", 1), ("G", 6),
    ("U", 5), ("FA", 0), ("CA", 1), ("FB-", 1), ("A", 6), ("CB", 5), ("T0", 0), ("A", 5), ("CA", 6), ("FB+", 7),
    ("FB-", 7), ("U", 6), ("P1", 0), ("CA", 5), ("G", 4), ("U", 4), ("CB", 6), ("FA", 1), ("FB+", 5), ("SA-", 0),
    ("G", 3), ("CB", 4), ("FB-", 5), ("U", 3), ("G", 2), ("FA", 6), ("U", 2), ("SA+", 0), ("A", 4), ("FB+", 6),
    ("A", 3), ("CB", 2), ("FA", 5), ("SA+", 1), ("FB-", 6), ("CA", 4), ("CA", 3), ("SB", 7), ("A", 2), ("SA-", 1),
    ("FB+", 1), ("A", 7), ("FB+", 4), ("CB", 3), ("CA", 2), ("FB-", 4), ("SB", 0), ("CA", 7), ("SA+", 6), ("FA", 4),
    ("SB", 5), ("SA-", 6), ("FB+", 2), ("FB-", 2), ("FA", 3), ("SA+", 5), ("SA-", 5), ("SB", 6), ("SB", 1),
    ("FA", 2), ("FB-", 3), ("FB+", 3), ("SB", 4), ("SA-", 4), ("SA+", 4), ("FA", 7), ("SB", 2), ("SA+", 3),
    ("SA-", 3), ("ACT", 5), ("SA+", 2), ("SA-", 2), ("SB", 3), ("SA+", 7), ("SA-", 7), ("ACT", 4), ("YA+", 5),
    ("YA-", 5), ("ACT", 2), ("YA+", 4), ("ACT", 3), ("YA-", 4), ("ZB", 4), ("ZF", 5), ("YA+", 2), ("YA-", 2),
    ("ZB", 2), ("YA-", 3), ("YA+", 3), ("ZB", 3), ("ZF", 4), ("YB+", 4), ("ZA", 5), ("YB-", 4), ("ACT", 1),
    ("ZF", 2), ("MIX", 5), ("YB-", 2), ("YB+", 2), ("ZF", 3), ("ACT", 6), ("YB+", 3), ("YB-", 3), ("ACT", 7),
    ("ZA", 4), ("YF", 4), ("YA+", 1), ("YA-", 1), ("MIX", 4), ("GI", 4), ("YF", 2), ("ZA", 2), ("ZB", 5),
    ("YA+", 6), ("YA-", 6), ("GI", 2), ("ZA", 3), ("MIX", 2), ("YF", 3), ("YA+", 7), ("YA-", 7), ("ZB", 6),
    ("MIX", 3), ("GI", 3), ("ZB", 7), ("ZF", 1), ("WA", 0), ("YB+", 5), ("YB-", 5), ("WA", 0), ("ZF", 6), ("ZF", 7),
    ("WA", 0), ("WA", 0), ("WA", 0), ("YB+", 6), ("YB-", 6), ("WA", 0), ("WA", 0), ("WA", 0), ("WA", 0), ("YB-", 7),
    ("YB+", 7), ("WA", 0), ("WA", 0), ("WA", 0), ("ZA", 1), ("YF", 5), ("ZB", 1), ("ACT", 0), ("YF", 6), ("MIX", 1),
    ("RS0", 0), ("GI", 5), ("ZA", 6), ("YF", 7), ("GI", 6), ("YA-", 0), ("YB-", 1), ("YA+", 0), ("YB+", 1),
    ("MIX", 6), ("ZA", 7), ("GI", 7), ("ZB", 0), ("MIX", 7), ("ZF", 0), ("WB", 0), ("WB", 0), ("YF", 1), ("WB", 0),
    ("WB", 0), ("WB", 0), ("WB", 0), ("YB+", 0), ("YB-", 0), ("GI", 1), ("RS1", 0), ("WB", 0), ("WB", 0), ("ZA", 0),
    ("WB", 0), ("WB", 0), ("WB", 0), ("YF", 0), ("MIX", 0), ("FI0", 0), ("WB", 0), ("GI", 0), ("FI1", 0),
)


def kernel(
    x_hbm, og_hbm, wg_hbm, wu_hbm, wd_hbm,
    h_out, gg_out, ug_out, xf_out, of_out, mix_out, gi_out, gate_out, up_out, down_out,
    xo, wg, wu, wd, wgt, wut, wdt, part, core_in, y1b, y2b, zb, za, y1a, y2a, full, mix, mix_in, mix_z, outs, sums,
    send_sem, recv_sem, load_sem, weight_sem, store_sem, tile_sem, out_sem,
):
    row, col = lax.axis_index("row"), lax.axis_index("col")
    x, zl = row // 2, row % 2
    zh, y, core = col // 8, (col // 2) % 4, col % 2
    zo, other = 1 - zh, 1 - core
    y_next, y_prev, y_far = (y + 1) % 4, (y + 3) % 4, (y + 2) % 4
    rows, width = x_hbm.shape
    hidden = wg_hbm.shape[1]
    half = hidden // 2
    low, high = slice(0, half // 2), slice(half // 2, half)
    pair = pl.ds(0, 2)

    def device(x=x, zl=zl, zh=zh, y=y, core=core):
        return {"row": x * 2 + zl, "col": zh * 8 + y * 2 + core}

    to_core = device(core=other)
    to_next, to_prev = device(y=y_next), device(y=y_prev)
    to_zh, to_zl = device(zh=zo), device(zl=1 - zl)

    def along(d):
        return device(x=(x + d) % 4)

    pending = []
    slots = {}
    seen = set()

    def remote(name, j, src, dst, target):
        k = slots.setdefault((name, j), len(slots))
        return pltpu.make_async_remote_copy(
            src_ref=src, dst_ref=dst, send_sem=send_sem.at[k], recv_sem=recv_sem.at[k],
            device_id=target, device_id_type=MESH,
        )

    def send(name, j, src, dst, target):
        copy = remote(name, j, src, dst, target)
        copy.start()
        pending.append(copy)

    def arrive(name, j, dst):
        if (name, j) not in seen:
            seen.add((name, j))
            remote(name, j, dst, dst, to_core).wait_recv()

    settled = []

    def settle(count):
        while len(settled) < count:
            copy = pending[len(settled)]
            copy.wait_send()
            settled.append(copy)

    stores = []

    def store(src, dst, sem):
        copy = pltpu.make_async_copy(src, dst, sem)
        copy.start()
        stores.append(copy)

    loads = [
        pltpu.make_async_copy(src, xo.at[0, i], load_sem.at[i])
        for i, src in enumerate((x_hbm, og_hbm))
    ]
    weights = [
        pltpu.make_async_copy(src, dst, weight_sem.at[i])
        for i, (src, dst) in enumerate(((wg_hbm, wg), (wu_hbm, wu), (wd_hbm, wd)))
    ]
    for copy in loads + weights:
        copy.start()

    barrier = pltpu.get_barrier_semaphore()
    to_next_zh, to_prev_zh = device(zh=zo, y=y_next), device(zh=zo, y=y_prev)
    peers = [to_core, to_next, to_prev, to_zh, to_zl, to_next_zh, to_prev_zh] + [along(d) for d in (1, 2, 3)]
    for peer in peers:
        pl.semaphore_signal(barrier, inc=1, device_id=peer, device_id_type=MESH)
    pl.semaphore_wait(barrier, len(peers))

    def row_own(i):
        loads[i].wait()
        mine = xo.at[0, i]
        send(f"row{i}", PAIR, mine, xo.at[PAIR, i], to_zl)
        for d in (1, 3, 2):
            j = OFFSETS.index((d, 0))
            send(f"row{i}", j, mine, xo.at[j, i], along(4 - d))

    def row_pair(i):
        theirs = xo.at[PAIR, i]
        arrive(f"row{i}", PAIR, theirs)
        for d in (1, 3, 2):
            j = OFFSETS.index((d, 1))
            send(f"row{i}", j, theirs, xo.at[j, i], along(4 - d))

    def transpose(src, dst):
        across = src.shape[0] < src.shape[1]
        size = max(src.shape) // 8
        for k in range(8):
            block = slice(k * size, (k + 1) * size)
            if across:
                dst[block, :] = src[:, block].T
            else:
                dst[:, block] = src[block, :].T

    def send_product(j, a):
        send(f"core_in{a}", j, part.at[j, other, :, :, a], core_in.at[j, :, :, a], to_core)

    def product(j, a, w, i):
        if j == 0:
            weights[a].wait()
            if a == 2:
                transpose(wd, wdt)
        else:
            arrive(f"row{i}", j, xo.at[j, i])
        left = xo[j, i]
        for c in range(2):
            cols = slice(c * half, (c + 1) * half)
            part[j, c, :, :, a] = dot(left, w[:, cols], NN).astype(BF16).reshape(4, 2, 16, half)
        send_product(j, a)
        if a != 1 and j < LATE:
            store(xo.at[j, i], (xf_out, of_out)[i].at[j], store_sem.at[i, 0, j])

    def add(j, yy, zz, arrays):
        part[j, core, yy, zz, arrays] += core_in[j, yy, zz, arrays]

    def core_pair(j):
        for a in range(2):
            arrive(f"core_in{a}", j, core_in.at[j, :, :, a])
        both = slice(0, 2)
        add(j, y_far, 0, both)
        send("y1b+", j, part.at[j, core, y_far, 0, pair], y1b.at[j, 0], to_next)
        add(j, y_far, 1, both)
        send("y1b-", j, part.at[j, core, y_far, 1, pair], y1b.at[j, 1], to_prev)
        add(j, y_next, 1, both)
        send("y2b+e", j, part.at[j, core, y_next, 1, pair], y2b.at[j, 0, 1], to_next)
        add(j, y_prev, 0, both)
        send("y2b-e", j, part.at[j, core, y_prev, 0, pair], y2b.at[j, 1, 0], to_prev)
        add(j, y_next, 0, both)
        add(j, y_prev, 1, both)
        add(j, y, 0, both)
        add(j, y, 1, both)

    def first_next(j):
        arrive("y1b+", j, y1b.at[j, 0])
        part[j, core, y_next, 0, 0:2] += y1b[j, 0]
        send("y2b+l", j, part.at[j, core, y_next, 0, pair], y2b.at[j, 0, 0], to_next)

    def first_prev(j):
        arrive("y1b-", j, y1b.at[j, 1])
        part[j, core, y_prev, 1, 0:2] += y1b[j, 1]
        send("y2b-l", j, part.at[j, core, y_prev, 1, pair], y2b.at[j, 1, 1], to_prev)

    def second_pair(j):
        arrive("y2b+e", j, y2b.at[j, 0, 1])
        arrive("y2b+l", j, y2b.at[j, 0, 0])
        arrive("y2b-e", j, y2b.at[j, 1, 0])
        arrive("y2b-l", j, y2b.at[j, 1, 1])
        total = part[j, core, y, zo, 0:2].astype(F32) + y2b[j, 0, zo].astype(F32)
        part[j, core, y, zo, 0:2] = (total + y2b[j, 1, zo].astype(F32)).astype(BF16)
        send("zb", j, part.at[j, core, y, zo, pair], zb.at[j], to_zh)

    def core_last(j):
        arrive("core_in2", j, core_in.at[j, :, :, 2])
        for yy in range(4):
            add(j, yy, zo, 2)
        send("za", j, part.at[j, core, :, zo, 2], za.at[j], to_zh)
        for yy in range(4):
            add(j, yy, zh, 2)

    def first_last(j):
        arrive("za", j, za.at[j])
        part[j, core, y_far, zh, 2] += za[j, y_far]
        send("y1a+", j, part.at[j, core, y_far, zh, 2, :, low], y1a.at[j, 0], to_next)
        send("y1a-", j, part.at[j, core, y_far, zh, 2, :, high], y1a.at[j, 1], to_prev)
        part[j, core, y_next, zh, 2] += za[j, y_next]
        part[j, core, y_prev, zh, 2] += za[j, y_prev]

    def second_next(j):
        arrive("y1a+", j, y1a.at[j, 0])
        part[j, core, y_next, zh, 2, :, low] += y1a[j, 0]
        send("y2a+", j, part.at[j, core, y_next, zh, 2], y2a.at[j, 0], to_next)

    def second_prev(j):
        arrive("y1a-", j, y1a.at[j, 1])
        part[j, core, y_prev, zh, 2, :, high] += y1a[j, 1]
        send("y2a-", j, part.at[j, core, y_prev, zh, 2], y2a.at[j, 1], to_prev)

    def activations(j):
        arrive("y2a+", j, y2a.at[j, 0])
        arrive("y2a-", j, y2a.at[j, 1])
        arrive("zb", j, zb.at[j])
        for cols in (low, high):

            def term(*values):
                total = values[0].astype(F32)
                for value in values[1:]:
                    total = total + value.astype(F32)
                return total

            gate, up = (
                term(
                    part[j, core, y, zh, a, :, cols], y2b[j, 0, zh, a, :, cols],
                    y2b[j, 1, zh, a, :, cols], zb[j, a, :, cols],
                )
                for a in range(2)
            )
            act_grad = term(
                part[j, core, y, zh, 2, :, cols], za[j, y, :, cols],
                y2a[j, 0, :, cols], y2a[j, 1, :, cols],
            )
            act, slope = silu_parts(gate)
            full[j, core, y, zh, 0, :, cols] = (act_grad * up * slope).astype(BF16)
            full[j, core, y, zh, 1, :, cols] = (act_grad * act).astype(BF16)
            full[j, core, y, zh, 2, :, cols] = (act * up).astype(BF16)
        mine, single = full.at[j, core, y, zh, pair], full.at[j, core, y, zh, 2]
        send("gzb", j, mine, mine, to_zh)
        send("gya+", j, single, single, to_next)
        send("gya-", j, single, single, to_prev)
        send("gyb+o", j, mine, mine, to_next)
        send("gyb-o", j, mine, mine, to_prev)
        if j in DIRECT:
            send("gyb+z", j, mine, mine, to_next_zh)
            send("gyb-z", j, mine, mine, to_prev_zh)
            send("gza_o", j, single, single, to_zh)

    def spread_z(j):
        theirs = full.at[j, core, y, zo, pair]
        arrive("gzb", j, theirs)
        if j not in DIRECT:
            send("gyb+z", j, theirs, theirs, to_next)
            send("gyb-z", j, theirs, theirs, to_prev)

    def spread_single(j, name, yy, cols, target):
        piece = full.at[j, core, yy, zh, 2]
        arrive("gya" + name, j, piece)
        send("gfa" + name, j, piece.at[:, cols], piece.at[:, cols], target)
        if j in DIRECT:
            send("gza" + name, j, piece, piece, to_zh)

    def spread_pair(j, name, yy, z, target):
        arrive(f"gyb{name}o", j, full.at[j, core, yy, zh, pair])
        arrive(f"gyb{name}z", j, full.at[j, core, yy, zo, pair])
        piece = full.at[j, core, yy, z, pair]
        send("gfb" + name, j, piece, piece, target)

    def far_single(j):
        far = full.at[j, core, y_far, zh, 2]
        arrive("gfa+", j, far.at[:, low])
        arrive("gfa-", j, far.at[:, high])
        if j in DIRECT:
            send("gza_f", j, far, far, to_zh)
        else:
            ring = full.at[j, core, :, zh, 2]
            send("gza", j, ring, ring, to_zh)

    def far_pair(j):
        arrive("gfb+", j, full.at[j, core, y_far, 0, pair])
        arrive("gfb-", j, full.at[j, core, y_far, 1, pair])
        whole = full.at[j, core, :, :, pair]
        send("gcb", j, whole, whole, to_core)

    def spread_rest(j):
        if j in DIRECT:
            for name, yy in (("gza_o", y), ("gza+", y_prev), ("gza-", y_next), ("gza_f", y_far)):
                arrive(name, j, full.at[j, core, yy, zo, 2])
        else:
            arrive("gza", j, full.at[j, core, :, zo, 2])
        whole = full.at[j, core, :, :, 2]
        send("gca", j, whole, whole, to_core)

    def send_mixed(j, i, value):
        mix[j, i] = value.astype(BF16)
        d = OFFSETS[j][0]
        if d:
            send(f"mix{i}", j, mix.at[j, i], mix_in.at[j - 2, i], along(d))

    def acts(j, c, a):
        return full[j, c, :, :, a].reshape(rows, half)

    def store_acts(j, a, dst):
        if j < LATE:
            for c in range(2):
                store(
                    full.at[j, c, :, :, a], dst.at[j, :, :, :, pl.ds(c * half, half)],
                    store_sem.at[2 + a, c, j],
                )

    def output_mixed(j):
        arrive("gca", j, full.at[j, other, :, :, 2])
        value = dot(acts(j, 0, 2), wd[0:half, :], NN) + dot(acts(j, 1, 2), wd[half:hidden, :], NN)
        send_mixed(j, 0, value)
        store_acts(j, 2, h_out)

    def output_grad(j):
        arrive("gcb", j, full.at[j, other, :, :, pair])
        value = dot(acts(j, 0, 0), wgt[0:half, :], NN) + dot(acts(j, 1, 0), wgt[half:hidden, :], NN)
        value = value + dot(acts(j, 0, 1), wut[0:half, :], NN) + dot(acts(j, 1, 1), wut[half:hidden, :], NN)
        send_mixed(j, 1, value)
        store_acts(j, 0, gg_out)
        store_acts(j, 1, ug_out)

    def row_total(i, e):
        total = mix[OFFSETS.index((0, e)), i].astype(F32)
        for d in (1, 2, 3):
            j = OFFSETS.index((d, e))
            arrive(f"mix{i}", j, mix_in.at[j - 2, i])
            total = total + mix_in[j - 2, i].astype(F32)
        return total

    def row_sum(i):
        mix[PAIR, i] = row_total(i, 1).astype(BF16)
        send(f"mix_z{i}", 0, mix.at[PAIR, i], mix_z.at[i], to_zl)

    def finish(i):
        total = row_total(i, 0)
        arrive(f"mix_z{i}", 0, mix_z.at[i])
        outs[i] = (total + mix_z[i].astype(F32)).astype(BF16)
        store(outs.at[i], (mix_out, gi_out)[i], out_sem.at[i])

    begun, done = [], []

    def weight_tile(k, first, end):
        tile = half // 2
        a, t = k // 4, k % 4
        units = full[first:end, t // 2, :, :, a, :, (low, high)[t % 2]].reshape((end - first) * rows, tile)
        side = xo[first:end, a // 2].reshape((end - first) * rows, width)
        value = dot(units, side, TN) if a == 2 else dot(side, units, TN)
        if first > LATE:
            value = value + sums[a, t].astype(F32)
        sums[a, t] = value.astype(PARTIAL)

    def weight_first():
        weight_tile(len(begun), LATE, SPLIT)
        begun.append(True)

    def weight_second():
        k = len(done)
        weight_tile(k, SPLIT, CHUNKS)
        copy = pltpu.make_async_copy(
            sums.at[k // 4, k % 4], (gate_out, up_out, down_out)[k // 4].at[k % 4], tile_sem.at[k]
        )
        copy.start()
        done.append(copy)

    stages = {
        "R0": lambda j: row_own(0), "R1": lambda j: row_own(1),
        "P0": lambda j: row_pair(0), "P1": lambda j: row_pair(1),
        "G": lambda j: product(j, 0, wg, 0),
        "U": lambda j: product(j, 1, wu, 0),
        "A": lambda j: product(j, 2, wdt, 1),
        "T0": lambda j: transpose(wg, wgt), "T1": lambda j: transpose(wu, wut),
        "CB": core_pair, "CA": core_last, "FB+": first_next, "FB-": first_prev, "FA": first_last,
        "SA+": second_next, "SA-": second_prev, "SB": second_pair, "ACT": activations, "ZB": spread_z,
        "YA+": lambda j: spread_single(j, "+", y_prev, low, to_next),
        "YA-": lambda j: spread_single(j, "-", y_next, high, to_prev),
        "YB+": lambda j: spread_pair(j, "+", y_prev, 0, to_next),
        "YB-": lambda j: spread_pair(j, "-", y_next, 1, to_prev),
        "ZF": far_single, "YF": far_pair, "ZA": spread_rest, "MIX": output_mixed, "GI": output_grad,
        "RS0": lambda j: row_sum(0), "RS1": lambda j: row_sum(1),
        "FI0": lambda j: finish(0), "FI1": lambda j: finish(1),
        "WA": lambda j: weight_first(), "WB": lambda j: weight_second(),
    }
    sent = []
    for name, j in ORDER:
        stages[name](j)
        sent.append(len(pending))
        if len(sent) > 40:
            settle(sent[-41])
    settle(len(pending))
    for copy in stores + done:
        copy.wait()


def exchange(inputs, gate_weight, up_weight, down_weight, out_grad):
    rows, width = inputs.shape
    hidden = gate_weight.shape[1]
    half = hidden // 2

    def buffer(*shape):
        return pltpu.VMEM(shape, BF16)

    def out(*shape, dtype=BF16):
        return jax.ShapeDtypeStruct(shape, dtype)

    wide = out(LATE, 4, 2, 16, hidden)
    thin = out(LATE, rows, width)
    own = out(rows, width)
    columns = out(4, width, hidden // 4, dtype=PARTIAL)
    any_space = pl.BlockSpec(memory_space=pl.ANY)
    outputs = (
        wide, wide, wide, thin, thin, own, own,
        columns, columns, out(4, hidden // 4, width, dtype=PARTIAL),
    )
    return pl.pallas_call(
        kernel,
        out_shape=outputs,
        in_specs=[any_space] * 5,
        out_specs=[any_space] * len(outputs),
        scratch_shapes=[
            buffer(CHUNKS, 2, rows, width),
            buffer(width, hidden),
            buffer(width, hidden),
            buffer(hidden, width),
            buffer(hidden, width),
            buffer(hidden, width),
            buffer(width, hidden),
            buffer(CHUNKS, 2, 4, 2, 3, 16, half),
            buffer(CHUNKS, 4, 2, 3, 16, half),
            buffer(CHUNKS, 2, 2, 16, half),
            buffer(CHUNKS, 2, 2, 2, 16, half),
            buffer(CHUNKS, 2, 16, half),
            buffer(CHUNKS, 4, 16, half),
            buffer(CHUNKS, 2, 16, half // 2),
            buffer(CHUNKS, 2, 16, half),
            buffer(CHUNKS, 2, 4, 2, 3, 16, half),
            buffer(CHUNKS, 2, rows, width),
            buffer(CHUNKS - 2, 2, rows, width),
            buffer(2, rows, width),
            buffer(2, rows, width),
            pltpu.VMEM((3, 4, width, hidden // 4), PARTIAL),
            pltpu.SemaphoreType.DMA((COPIES,)),
            pltpu.SemaphoreType.DMA((COPIES,)),
            pltpu.SemaphoreType.DMA((2,)),
            pltpu.SemaphoreType.DMA((3,)),
            pltpu.SemaphoreType.DMA((5, 2, LATE)),
            pltpu.SemaphoreType.DMA((12,)),
            pltpu.SemaphoreType.DMA((2,)),
        ],
        compiler_params=pltpu.CompilerParams(
            collective_id=0, has_side_effects=True, vmem_limit_bytes=VMEM_LIMIT
        ),
    )(inputs, out_grad, gate_weight, up_weight, down_weight)


def weight_kernel(
    x_hbm, og_hbm, gg_hbm, ug_hbm, h_hbm, gate_hbm, up_hbm, down_hbm, mix_hbm, gi_hbm,
    mix_out, gi_out, gate_out, up_out, down_out,
    x, og, acts, parts, wide, tall, own, left_sem, part_sem, out_sem, own_sem,
):
    tiles, tile = wide.shape[1], wide.shape[3]
    pieces = ((x_hbm, x), (og_hbm, og), (gg_hbm, acts.at[0]), (ug_hbm, acts.at[1]), (h_hbm, acts.at[2]))
    loads = [pltpu.make_async_copy(src, dst, left_sem.at[i]) for i, (src, dst) in enumerate(pieces)]
    mine = [pltpu.make_async_copy(src, own.at[i], own_sem.at[i]) for i, src in enumerate((mix_hbm, gi_hbm))]
    sums = [
        [pltpu.make_async_copy(src.at[t], parts.at[a, t], part_sem.at[a, t]) for t in range(tiles)]
        for a, src in enumerate((gate_hbm, up_hbm, down_hbm))
    ]
    order = ((0, (0, 2)), (1, (3,)), (2, (1, 4)))
    for a, needs in order:
        for i in needs:
            loads[i].start()
        for copy in sums[a]:
            copy.start()
    for copy in mine:
        copy.start()
    stores = []
    for a, needs in order:
        for i in needs:
            loads[i].wait()
        for t in range(tiles):
            cols = slice(t * tile, (t + 1) * tile)
            sums[a][t].wait()
            if a == 2:
                tall[cols, :] = parts[a, t].astype(F32) + dot(acts[2, :, cols], og[...], TN)
                src, dst = tall.at[pl.ds(t * tile, tile)], down_out.at[pl.ds(t * tile, tile)]
            else:
                wide[a, t] = parts[a, t].astype(F32) + dot(x[...], acts[a, :, cols], TN)
                src, dst = wide.at[a, t], (gate_out, up_out)[a].at[:, pl.ds(t * tile, tile)]
            stores.append(pltpu.make_async_copy(src, dst, out_sem.at[a, t]))
            stores[-1].start()
    for i, copy in enumerate(mine):
        copy.wait()
        stores.append(pltpu.make_async_copy(own.at[i], (mix_out, gi_out)[i], own_sem.at[2 + i]))
        stores[-1].start()
    for copy in stores:
        copy.wait()


def weight_grads(x, og, gg, ug, h, gate_part, up_part, down_part, mixed, grad_input):
    tokens, width = x.shape
    hidden = h.shape[1]
    tiles = gate_part.shape[0]
    tile = hidden // tiles
    any_space = pl.BlockSpec(memory_space=pl.ANY)
    return pl.pallas_call(
        weight_kernel,
        out_shape=(
            jax.ShapeDtypeStruct(mixed.shape, BF16),
            jax.ShapeDtypeStruct(mixed.shape, BF16),
            jax.ShapeDtypeStruct((width, hidden), F32),
            jax.ShapeDtypeStruct((width, hidden), F32),
            jax.ShapeDtypeStruct((hidden, width), F32),
        ),
        in_specs=[any_space] * 10,
        out_specs=[any_space] * 5,
        scratch_shapes=[
            pltpu.VMEM((tokens, width), BF16),
            pltpu.VMEM((tokens, width), BF16),
            pltpu.VMEM((3, tokens, hidden), BF16),
            pltpu.VMEM((3, tiles, width, tile), PARTIAL),
            pltpu.VMEM((2, tiles, width, tile), F32),
            pltpu.VMEM((hidden, width), F32),
            pltpu.VMEM((2,) + mixed.shape, BF16),
            pltpu.SemaphoreType.DMA((5,)),
            pltpu.SemaphoreType.DMA((3, tiles)),
            pltpu.SemaphoreType.DMA((3, tiles)),
            pltpu.SemaphoreType.DMA((4,)),
        ],
        compiler_params=pltpu.CompilerParams(vmem_limit_bytes=VMEM_LIMIT),
    )(x, og, gg, ug, h, gate_part, up_part, down_part, mixed, grad_input)


def body(inputs, gate_weight, up_weight, down_weight, out_grad):
    h, gg, ug, x, og, mixed, grad_input, gate_part, up_part, down_part = exchange(
        inputs, gate_weight, up_weight, down_weight, out_grad
    )
    width = inputs.shape[1]
    hidden = gate_weight.shape[1]
    return weight_grads(
        x.reshape(-1, width), og.reshape(-1, width),
        gg.reshape(-1, hidden), ug.reshape(-1, hidden), h.reshape(-1, hidden),
        gate_part, up_part, down_part, mixed, grad_input,
    )


def solution(mesh):
    in_specs = (P("row", "col"), P("col", "row"), P("col", "row"), P("row", "col"), P("row", "col"))
    out_specs = (
        P("row", "col"),
        P("row", "col"),
        P("col", "row"),
        P("col", "row"),
        P("row", "col"),
    )
    return jax.shard_map(body, mesh=mesh, in_specs=in_specs, out_specs=out_specs, check_vma=False)
```

```python
import functools

import jax
import jax.numpy as jnp
from jax import lax
from jax.experimental import pallas as pl
from jax.experimental.pallas import tpu as pltpu
from jax.sharding import PartitionSpec as P

MESH = pl.DeviceIdType.MESH
BF16, F32 = jnp.bfloat16, jnp.float32
PARTIAL = BF16
OFFSETS = ((0, 0), (0, 1), (2, 1), (1, 1), (3, 1), (2, 0), (1, 0), (3, 0))
CHUNKS = len(OFFSETS)
PAIR = OFFSETS.index((0, 1))
LATE = 2
SPLIT = 5
DIRECT = ()
COPIES = 270
VMEM_LIMIT = 62 << 20
NN = (((1,), (0,)), ((), ()))
TN = (((0,), (0,)), ((), ()))


def dot(left, right, dims):
    return lax.dot_general(left, right, dims, preferred_element_type=F32)


def silu_parts(gate):
    sig = jax.nn.sigmoid(gate)
    return gate * sig, sig * (1.0 + gate * (1.0 - sig))


ORDER = (
    ("R0", 0), ("G", 0), ("U", 0), ("CB", 0), ("R1", 0), ("A", 0), ("G", 7), ("U", 7), ("CA", 0), ("FB+", 0),
    ("FB-", 0), ("G", 1), ("CB", 7), ("U", 1), ("P0", 0), ("G", 6), ("A", 1), ("CB", 1), ("A", 7), ("FB+", 7),
    ("U", 6), ("CA", 7), ("A", 6), ("P1", 0), ("FB-", 7), ("SB", 0), ("CB", 6), ("FB-", 1), ("A", 5), ("CA", 1),
    ("CA", 6), ("G", 3), ("FB+", 1), ("CA", 5), ("G", 5), ("U", 5), ("FB+", 6), ("FB-", 6), ("U", 3), ("CB", 5),
    ("G", 4), ("G", 2), ("CB", 3), ("U", 2), ("A", 3), ("U", 4), ("T1", 0), ("A", 4), ("CA", 3), ("FA", 6),
    ("CB", 4), ("FB-", 3), ("SB", 6), ("FA", 1), ("FB+", 3), ("FA", 5), ("CA", 4), ("CB", 2), ("A", 2), ("FA", 3),
    ("CA", 2), ("SB", 1), ("FB+", 4), ("SB", 3), ("FB-", 4), ("FB+", 2), ("FB-", 2), ("FA", 4), ("SA+", 3),
    ("SA+", 5), ("SA-", 3), ("FA", 2), ("SB", 7), ("SA-", 6), ("FB+", 5), ("FB-", 5), ("SB", 4), ("SB", 2),
    ("SA-", 4), ("SA+", 4), ("ACT", 3), ("SA+", 2), ("SA-", 2), ("SB", 5), ("SA-", 1), ("YA+", 3), ("SA+", 1),
    ("YA-", 3), ("ACT", 4), ("FA", 7), ("ACT", 2), ("ZF", 3), ("YA-", 4), ("YA+", 4), ("SA-", 5), ("ACT", 1),
    ("SA+", 7), ("YA-", 2), ("ZF", 4), ("YA+", 2), ("ZB", 4), ("ZA", 3), ("YA+", 1), ("YA-", 1), ("ACT", 5),
    ("MIX", 3), ("ZB", 2), ("ZF", 2), ("ZB", 3), ("YB+", 4), ("SA-", 7), ("ZF", 1), ("YA+", 5), ("ZA", 4),
    ("SA+", 6), ("YB-", 4), ("T0", 0), ("MIX", 4), ("YA-", 5), ("YB-", 2), ("YB+", 2), ("YB+", 3), ("ZA", 2),
    ("YB-", 3), ("ACT", 7), ("FA", 0), ("MIX", 2), ("YF", 4), ("ZF", 5), ("ACT", 6), ("ZA", 1), ("YF", 2),
    ("GI", 4), ("YF", 3), ("MIX", 1), ("YA+", 7), ("GI", 2), ("YA-", 7), ("ZB", 5), ("GI", 3), ("YA-", 6),
    ("ZA", 5), ("YA+", 6), ("ZB", 7), ("WA", 0), ("ZF", 7), ("MIX", 5), ("ZB", 6), ("SA-", 0), ("SA+", 0),
    ("YB-", 5), ("YB+", 5), ("WA", 0), ("ZF", 6), ("WA", 0), ("WA", 0), ("ZB", 1), ("WA", 0), ("YB+", 7),
    ("YB-", 7), ("WA", 0), ("WA", 0), ("YB+", 6), ("WA", 0), ("YB-", 6), ("ACT", 0), ("ZA", 7), ("WA", 0),
    ("RS0", 0), ("YF", 5), ("WA", 0), ("MIX", 7), ("YB-", 1), ("ZA", 6), ("WA", 0), ("WA", 0), ("YF", 7), ("GI", 5),
    ("YB+", 1), ("YF", 6), ("MIX", 6), ("YA-", 0), ("YA+", 0), ("ZB", 0), ("GI", 7), ("GI", 6), ("WB", 0),
    ("YF", 1), ("WB", 0), ("ZF", 0), ("WB", 0), ("WB", 0), ("YB+", 0), ("YB-", 0), ("GI", 1), ("WB", 0), ("RS1", 0),
    ("WB", 0), ("WB", 0), ("WB", 0), ("YF", 0), ("WB", 0), ("WB", 0), ("ZA", 0), ("WB", 0), ("WB", 0), ("GI", 0),
    ("MIX", 0), ("FI0", 0), ("FI1", 0),
)


def kernel(
    x_hbm, og_hbm, wg_hbm, wu_hbm, wd_hbm,
    h_out, gg_out, ug_out, xf_out, of_out, mix_out, gi_out, gate_out, up_out, down_out,
    xo, wg, wu, wd, wgt, wut, wdt, part, core_in, y1b, y2b, zb, za, y1a, y2a, full, mix, mix_in, mix_z, outs, sums,
    send_sem, recv_sem, load_sem, weight_sem, store_sem, tile_sem, out_sem,
):
    row, col = lax.axis_index("row"), lax.axis_index("col")
    x, zl = row // 2, row % 2
    zh, y, core = col // 8, (col // 2) % 4, col % 2
    zo, other = 1 - zh, 1 - core
    y_next, y_prev, y_far = (y + 1) % 4, (y + 3) % 4, (y + 2) % 4
    rows, width = x_hbm.shape
    hidden = wg_hbm.shape[1]
    half = hidden // 2
    low, high = slice(0, half // 2), slice(half // 2, half)
    pair = pl.ds(0, 2)

    def device(x=x, zl=zl, zh=zh, y=y, core=core):
        return {"row": x * 2 + zl, "col": zh * 8 + y * 2 + core}

    to_core = device(core=other)
    to_next, to_prev = device(y=y_next), device(y=y_prev)
    to_zh, to_zl = device(zh=zo), device(zl=1 - zl)

    def along(d):
        return device(x=(x + d) % 4)

    pending = []
    slots = {}
    seen = set()

    def remote(name, j, src, dst, target):
        k = slots.setdefault((name, j), len(slots))
        return pltpu.make_async_remote_copy(
            src_ref=src, dst_ref=dst, send_sem=send_sem.at[k], recv_sem=recv_sem.at[k],
            device_id=target, device_id_type=MESH,
        )

    def send(name, j, src, dst, target):
        copy = remote(name, j, src, dst, target)
        copy.start()
        pending.append(copy)

    def arrive(name, j, dst):
        if (name, j) not in seen:
            seen.add((name, j))
            remote(name, j, dst, dst, to_core).wait_recv()

    settled = []

    def settle(count):
        while len(settled) < count:
            copy = pending[len(settled)]
            copy.wait_send()
            settled.append(copy)

    stores = []

    def store(src, dst, sem):
        copy = pltpu.make_async_copy(src, dst, sem)
        copy.start()
        stores.append(copy)

    loads = [
        pltpu.make_async_copy(src, xo.at[0, i], load_sem.at[i])
        for i, src in enumerate((x_hbm, og_hbm))
    ]
    weights = [
        pltpu.make_async_copy(src, dst, weight_sem.at[i])
        for i, (src, dst) in enumerate(((wg_hbm, wg), (wu_hbm, wu), (wd_hbm, wd)))
    ]
    for copy in loads + weights:
        copy.start()

    barrier = pltpu.get_barrier_semaphore()
    to_next_zh, to_prev_zh = device(zh=zo, y=y_next), device(zh=zo, y=y_prev)
    peers = [to_core, to_next, to_prev, to_zh, to_zl, to_next_zh, to_prev_zh] + [along(d) for d in (1, 2, 3)]
    for peer in peers:
        pl.semaphore_signal(barrier, inc=1, device_id=peer, device_id_type=MESH)
    pl.semaphore_wait(barrier, len(peers))

    def row_own(i):
        loads[i].wait()
        mine = xo.at[0, i]
        send(f"row{i}", PAIR, mine, xo.at[PAIR, i], to_zl)
        for d in (1, 3, 2):
            j = OFFSETS.index((d, 0))
            send(f"row{i}", j, mine, xo.at[j, i], along(4 - d))

    def row_pair(i):
        theirs = xo.at[PAIR, i]
        arrive(f"row{i}", PAIR, theirs)
        for d in (1, 3, 2):
            j = OFFSETS.index((d, 1))
            send(f"row{i}", j, theirs, xo.at[j, i], along(4 - d))

    def transpose(src, dst):
        across = src.shape[0] < src.shape[1]
        size = max(src.shape) // 8
        for k in range(8):
            block = slice(k * size, (k + 1) * size)
            if across:
                dst[block, :] = src[:, block].T
            else:
                dst[:, block] = src[block, :].T

    def send_product(j, a):
        send(f"core_in{a}", j, part.at[j, other, :, :, a], core_in.at[j, :, :, a], to_core)

    def product(j, a, w, i):
        if j == 0:
            weights[a].wait()
            if a == 2:
                transpose(wd, wdt)
        else:
            arrive(f"row{i}", j, xo.at[j, i])
        left = xo[j, i]
        for c in range(2):
            cols = slice(c * half, (c + 1) * half)
            part[j, c, :, :, a] = dot(left, w[:, cols], NN).astype(BF16).reshape(4, 2, 16, half)
        send_product(j, a)
        if a != 1 and j < LATE:
            store(xo.at[j, i], (xf_out, of_out)[i].at[j], store_sem.at[i, 0, j])

    def add(j, yy, zz, arrays):
        part[j, core, yy, zz, arrays] += core_in[j, yy, zz, arrays]

    def core_pair(j):
        for a in range(2):
            arrive(f"core_in{a}", j, core_in.at[j, :, :, a])
        both = slice(0, 2)
        add(j, y_far, 0, both)
        send("y1b+", j, part.at[j, core, y_far, 0, pair], y1b.at[j, 0], to_next)
        add(j, y_far, 1, both)
        send("y1b-", j, part.at[j, core, y_far, 1, pair], y1b.at[j, 1], to_prev)
        add(j, y_next, 1, both)
        send("y2b+e", j, part.at[j, core, y_next, 1, pair], y2b.at[j, 0, 1], to_next)
        add(j, y_prev, 0, both)
        send("y2b-e", j, part.at[j, core, y_prev, 0, pair], y2b.at[j, 1, 0], to_prev)
        add(j, y_next, 0, both)
        add(j, y_prev, 1, both)
        add(j, y, 0, both)
        add(j, y, 1, both)

    def first_next(j):
        arrive("y1b+", j, y1b.at[j, 0])
        part[j, core, y_next, 0, 0:2] += y1b[j, 0]
        send("y2b+l", j, part.at[j, core, y_next, 0, pair], y2b.at[j, 0, 0], to_next)

    def first_prev(j):
        arrive("y1b-", j, y1b.at[j, 1])
        part[j, core, y_prev, 1, 0:2] += y1b[j, 1]
        send("y2b-l", j, part.at[j, core, y_prev, 1, pair], y2b.at[j, 1, 1], to_prev)

    def second_pair(j):
        arrive("y2b+e", j, y2b.at[j, 0, 1])
        arrive("y2b+l", j, y2b.at[j, 0, 0])
        arrive("y2b-e", j, y2b.at[j, 1, 0])
        arrive("y2b-l", j, y2b.at[j, 1, 1])
        total = part[j, core, y, zo, 0:2].astype(F32) + y2b[j, 0, zo].astype(F32)
        part[j, core, y, zo, 0:2] = (total + y2b[j, 1, zo].astype(F32)).astype(BF16)
        send("zb", j, part.at[j, core, y, zo, pair], zb.at[j], to_zh)

    def core_last(j):
        arrive("core_in2", j, core_in.at[j, :, :, 2])
        for yy in range(4):
            add(j, yy, zo, 2)
        send("za", j, part.at[j, core, :, zo, 2], za.at[j], to_zh)
        for yy in range(4):
            add(j, yy, zh, 2)

    def first_last(j):
        arrive("za", j, za.at[j])
        part[j, core, y_far, zh, 2] += za[j, y_far]
        send("y1a+", j, part.at[j, core, y_far, zh, 2, :, low], y1a.at[j, 0], to_next)
        send("y1a-", j, part.at[j, core, y_far, zh, 2, :, high], y1a.at[j, 1], to_prev)
        part[j, core, y_next, zh, 2] += za[j, y_next]
        part[j, core, y_prev, zh, 2] += za[j, y_prev]

    def second_next(j):
        arrive("y1a+", j, y1a.at[j, 0])
        part[j, core, y_next, zh, 2, :, low] += y1a[j, 0]
        send("y2a+", j, part.at[j, core, y_next, zh, 2], y2a.at[j, 0], to_next)

    def second_prev(j):
        arrive("y1a-", j, y1a.at[j, 1])
        part[j, core, y_prev, zh, 2, :, high] += y1a[j, 1]
        send("y2a-", j, part.at[j, core, y_prev, zh, 2], y2a.at[j, 1], to_prev)

    def activations(j):
        arrive("y2a+", j, y2a.at[j, 0])
        arrive("y2a-", j, y2a.at[j, 1])
        arrive("zb", j, zb.at[j])
        for cols in (low, high):

            def term(*values):
                total = values[0].astype(F32)
                for value in values[1:]:
                    total = total + value.astype(F32)
                return total

            gate, up = (
                term(
                    part[j, core, y, zh, a, :, cols], y2b[j, 0, zh, a, :, cols],
                    y2b[j, 1, zh, a, :, cols], zb[j, a, :, cols],
                )
                for a in range(2)
            )
            act_grad = term(
                part[j, core, y, zh, 2, :, cols], za[j, y, :, cols],
                y2a[j, 0, :, cols], y2a[j, 1, :, cols],
            )
            act, slope = silu_parts(gate)
            full[j, core, y, zh, 0, :, cols] = (act_grad * up * slope).astype(BF16)
            full[j, core, y, zh, 1, :, cols] = (act_grad * act).astype(BF16)
            full[j, core, y, zh, 2, :, cols] = (act * up).astype(BF16)
        mine, single = full.at[j, core, y, zh, pair], full.at[j, core, y, zh, 2]
        send("gzb", j, mine, mine, to_zh)
        send("gya+", j, single, single, to_next)
        send("gya-", j, single, single, to_prev)
        send("gyb+o", j, mine, mine, to_next)
        send("gyb-o", j, mine, mine, to_prev)
        if j in DIRECT:
            send("gyb+z", j, mine, mine, to_next_zh)
            send("gyb-z", j, mine, mine, to_prev_zh)
            send("gza_o", j, single, single, to_zh)

    def spread_z(j):
        theirs = full.at[j, core, y, zo, pair]
        arrive("gzb", j, theirs)
        if j not in DIRECT:
            send("gyb+z", j, theirs, theirs, to_next)
            send("gyb-z", j, theirs, theirs, to_prev)

    def spread_single(j, name, yy, cols, target):
        piece = full.at[j, core, yy, zh, 2]
        arrive("gya" + name, j, piece)
        send("gfa" + name, j, piece.at[:, cols], piece.at[:, cols], target)
        if j in DIRECT:
            send("gza" + name, j, piece, piece, to_zh)

    def spread_pair(j, name, yy, z, target):
        arrive(f"gyb{name}o", j, full.at[j, core, yy, zh, pair])
        arrive(f"gyb{name}z", j, full.at[j, core, yy, zo, pair])
        piece = full.at[j, core, yy, z, pair]
        send("gfb" + name, j, piece, piece, target)

    def far_single(j):
        far = full.at[j, core, y_far, zh, 2]
        arrive("gfa+", j, far.at[:, low])
        arrive("gfa-", j, far.at[:, high])
        if j in DIRECT:
            send("gza_f", j, far, far, to_zh)
        else:
            ring = full.at[j, core, :, zh, 2]
            send("gza", j, ring, ring, to_zh)

    def far_pair(j):
        arrive("gfb+", j, full.at[j, core, y_far, 0, pair])
        arrive("gfb-", j, full.at[j, core, y_far, 1, pair])
        whole = full.at[j, core, :, :, pair]
        send("gcb", j, whole, whole, to_core)

    def spread_rest(j):
        if j in DIRECT:
            for name, yy in (("gza_o", y), ("gza+", y_prev), ("gza-", y_next), ("gza_f", y_far)):
                arrive(name, j, full.at[j, core, yy, zo, 2])
        else:
            arrive("gza", j, full.at[j, core, :, zo, 2])
        whole = full.at[j, core, :, :, 2]
        send("gca", j, whole, whole, to_core)

    def send_mixed(j, i, value):
        mix[j, i] = value.astype(BF16)
        d = OFFSETS[j][0]
        if d:
            send(f"mix{i}", j, mix.at[j, i], mix_in.at[j - 2, i], along(d))

    def acts(j, c, a):
        return full[j, c, :, :, a].reshape(rows, half)

    def store_acts(j, a, dst):
        if j < LATE:
            for c in range(2):
                store(
                    full.at[j, c, :, :, a], dst.at[j, :, :, :, pl.ds(c * half, half)],
                    store_sem.at[2 + a, c, j],
                )

    def output_mixed(j):
        arrive("gca", j, full.at[j, other, :, :, 2])
        value = dot(acts(j, 0, 2), wd[0:half, :], NN) + dot(acts(j, 1, 2), wd[half:hidden, :], NN)
        send_mixed(j, 0, value)
        store_acts(j, 2, h_out)

    def output_grad(j):
        arrive("gcb", j, full.at[j, other, :, :, pair])
        value = dot(acts(j, 0, 0), wgt[0:half, :], NN) + dot(acts(j, 1, 0), wgt[half:hidden, :], NN)
        value = value + dot(acts(j, 0, 1), wut[0:half, :], NN) + dot(acts(j, 1, 1), wut[half:hidden, :], NN)
        send_mixed(j, 1, value)
        store_acts(j, 0, gg_out)
        store_acts(j, 1, ug_out)

    def row_total(i, e):
        total = mix[OFFSETS.index((0, e)), i].astype(F32)
        for d in (1, 2, 3):
            j = OFFSETS.index((d, e))
            arrive(f"mix{i}", j, mix_in.at[j - 2, i])
            total = total + mix_in[j - 2, i].astype(F32)
        return total

    def row_sum(i):
        mix[PAIR, i] = row_total(i, 1).astype(BF16)
        send(f"mix_z{i}", 0, mix.at[PAIR, i], mix_z.at[i], to_zl)

    def finish(i):
        total = row_total(i, 0)
        arrive(f"mix_z{i}", 0, mix_z.at[i])
        outs[i] = (total + mix_z[i].astype(F32)).astype(BF16)
        store(outs.at[i], (mix_out, gi_out)[i], out_sem.at[i])

    begun, done = [], []

    def weight_tile(k, first, end):
        tile = half // 2
        a, t = k // 4, k % 4
        units = full[first:end, t // 2, :, :, a, :, (low, high)[t % 2]].reshape((end - first) * rows, tile)
        side = xo[first:end, a // 2].reshape((end - first) * rows, width)
        value = dot(units, side, TN) if a == 2 else dot(side, units, TN)
        if first > LATE:
            value = value + sums[a, t].astype(F32)
        sums[a, t] = value.astype(PARTIAL)

    def weight_first():
        weight_tile(len(begun), LATE, SPLIT)
        begun.append(True)

    def weight_second():
        k = len(done)
        weight_tile(k, SPLIT, CHUNKS)
        copy = pltpu.make_async_copy(
            sums.at[k // 4, k % 4], (gate_out, up_out, down_out)[k // 4].at[k % 4], tile_sem.at[k]
        )
        copy.start()
        done.append(copy)

    stages = {
        "R0": lambda j: row_own(0), "R1": lambda j: row_own(1),
        "P0": lambda j: row_pair(0), "P1": lambda j: row_pair(1),
        "G": lambda j: product(j, 0, wg, 0),
        "U": lambda j: product(j, 1, wu, 0),
        "A": lambda j: product(j, 2, wdt, 1),
        "T0": lambda j: transpose(wg, wgt), "T1": lambda j: transpose(wu, wut),
        "CB": core_pair, "CA": core_last, "FB+": first_next, "FB-": first_prev, "FA": first_last,
        "SA+": second_next, "SA-": second_prev, "SB": second_pair, "ACT": activations, "ZB": spread_z,
        "YA+": lambda j: spread_single(j, "+", y_prev, low, to_next),
        "YA-": lambda j: spread_single(j, "-", y_next, high, to_prev),
        "YB+": lambda j: spread_pair(j, "+", y_prev, 0, to_next),
        "YB-": lambda j: spread_pair(j, "-", y_next, 1, to_prev),
        "ZF": far_single, "YF": far_pair, "ZA": spread_rest, "MIX": output_mixed, "GI": output_grad,
        "RS0": lambda j: row_sum(0), "RS1": lambda j: row_sum(1),
        "FI0": lambda j: finish(0), "FI1": lambda j: finish(1),
        "WA": lambda j: weight_first(), "WB": lambda j: weight_second(),
    }
    sent = []
    for name, j in ORDER:
        stages[name](j)
        sent.append(len(pending))
        if len(sent) > 40:
            settle(sent[-41])
    settle(len(pending))
    for copy in stores + done:
        copy.wait()


def exchange(inputs, gate_weight, up_weight, down_weight, out_grad):
    rows, width = inputs.shape
    hidden = gate_weight.shape[1]
    half = hidden // 2

    def buffer(*shape):
        return pltpu.VMEM(shape, BF16)

    def out(*shape, dtype=BF16):
        return jax.ShapeDtypeStruct(shape, dtype)

    wide = out(LATE, 4, 2, 16, hidden)
    thin = out(LATE, rows, width)
    own = out(rows, width)
    columns = out(4, width, hidden // 4, dtype=PARTIAL)
    any_space = pl.BlockSpec(memory_space=pl.ANY)
    outputs = (
        wide, wide, wide, thin, thin, own, own,
        columns, columns, out(4, hidden // 4, width, dtype=PARTIAL),
    )
    return pl.pallas_call(
        kernel,
        out_shape=outputs,
        in_specs=[any_space] * 5,
        out_specs=[any_space] * len(outputs),
        scratch_shapes=[
            buffer(CHUNKS, 2, rows, width),
            buffer(width, hidden),
            buffer(width, hidden),
            buffer(hidden, width),
            buffer(hidden, width),
            buffer(hidden, width),
            buffer(width, hidden),
            buffer(CHUNKS, 2, 4, 2, 3, 16, half),
            buffer(CHUNKS, 4, 2, 3, 16, half),
            buffer(CHUNKS, 2, 2, 16, half),
            buffer(CHUNKS, 2, 2, 2, 16, half),
            buffer(CHUNKS, 2, 16, half),
            buffer(CHUNKS, 4, 16, half),
            buffer(CHUNKS, 2, 16, half // 2),
            buffer(CHUNKS, 2, 16, half),
            buffer(CHUNKS, 2, 4, 2, 3, 16, half),
            buffer(CHUNKS, 2, rows, width),
            buffer(CHUNKS - 2, 2, rows, width),
            buffer(2, rows, width),
            buffer(2, rows, width),
            pltpu.VMEM((3, 4, width, hidden // 4), PARTIAL),
            pltpu.SemaphoreType.DMA((COPIES,)),
            pltpu.SemaphoreType.DMA((COPIES,)),
            pltpu.SemaphoreType.DMA((2,)),
            pltpu.SemaphoreType.DMA((3,)),
            pltpu.SemaphoreType.DMA((5, 2, LATE)),
            pltpu.SemaphoreType.DMA((12,)),
            pltpu.SemaphoreType.DMA((2,)),
        ],
        compiler_params=pltpu.CompilerParams(
            collective_id=0, has_side_effects=True, vmem_limit_bytes=VMEM_LIMIT
        ),
    )(inputs, out_grad, gate_weight, up_weight, down_weight)


def weight_kernel(
    x_hbm, og_hbm, gg_hbm, ug_hbm, h_hbm, gate_hbm, up_hbm, down_hbm, mix_hbm, gi_hbm,
    mix_out, gi_out, gate_out, up_out, down_out,
    x, og, acts, parts, wide, tall, own, left_sem, part_sem, out_sem, own_sem,
):
    tiles, tile = wide.shape[1], wide.shape[3]
    pieces = ((x_hbm, x), (og_hbm, og), (gg_hbm, acts.at[0]), (ug_hbm, acts.at[1]), (h_hbm, acts.at[2]))
    loads = [pltpu.make_async_copy(src, dst, left_sem.at[i]) for i, (src, dst) in enumerate(pieces)]
    mine = [pltpu.make_async_copy(src, own.at[i], own_sem.at[i]) for i, src in enumerate((mix_hbm, gi_hbm))]
    sums = [
        [pltpu.make_async_copy(src.at[t], parts.at[a, t], part_sem.at[a, t]) for t in range(tiles)]
        for a, src in enumerate((gate_hbm, up_hbm, down_hbm))
    ]
    order = ((0, (0, 2)), (1, (3,)), (2, (1, 4)))
    for a, needs in order:
        for i in needs:
            loads[i].start()
        for copy in sums[a]:
            copy.start()
    for copy in mine:
        copy.start()
    stores = []
    for a, needs in order:
        for i in needs:
            loads[i].wait()
        for t in range(tiles):
            cols = slice(t * tile, (t + 1) * tile)
            sums[a][t].wait()
            if a == 2:
                tall[cols, :] = parts[a, t].astype(F32) + dot(acts[2, :, cols], og[...], TN)
                src, dst = tall.at[pl.ds(t * tile, tile)], down_out.at[pl.ds(t * tile, tile)]
            else:
                wide[a, t] = parts[a, t].astype(F32) + dot(x[...], acts[a, :, cols], TN)
                src, dst = wide.at[a, t], (gate_out, up_out)[a].at[:, pl.ds(t * tile, tile)]
            stores.append(pltpu.make_async_copy(src, dst, out_sem.at[a, t]))
            stores[-1].start()
    for i, copy in enumerate(mine):
        copy.wait()
        stores.append(pltpu.make_async_copy(own.at[i], (mix_out, gi_out)[i], own_sem.at[2 + i]))
        stores[-1].start()
    for copy in stores:
        copy.wait()


def weight_grads(x, og, gg, ug, h, gate_part, up_part, down_part, mixed, grad_input):
    tokens, width = x.shape
    hidden = h.shape[1]
    tiles = gate_part.shape[0]
    tile = hidden // tiles
    any_space = pl.BlockSpec(memory_space=pl.ANY)
    return pl.pallas_call(
        weight_kernel,
        out_shape=(
            jax.ShapeDtypeStruct(mixed.shape, BF16),
            jax.ShapeDtypeStruct(mixed.shape, BF16),
            jax.ShapeDtypeStruct((width, hidden), F32),
            jax.ShapeDtypeStruct((width, hidden), F32),
            jax.ShapeDtypeStruct((hidden, width), F32),
        ),
        in_specs=[any_space] * 10,
        out_specs=[any_space] * 5,
        scratch_shapes=[
            pltpu.VMEM((tokens, width), BF16),
            pltpu.VMEM((tokens, width), BF16),
            pltpu.VMEM((3, tokens, hidden), BF16),
            pltpu.VMEM((3, tiles, width, tile), PARTIAL),
            pltpu.VMEM((2, tiles, width, tile), F32),
            pltpu.VMEM((hidden, width), F32),
            pltpu.VMEM((2,) + mixed.shape, BF16),
            pltpu.SemaphoreType.DMA((5,)),
            pltpu.SemaphoreType.DMA((3, tiles)),
            pltpu.SemaphoreType.DMA((3, tiles)),
            pltpu.SemaphoreType.DMA((4,)),
        ],
        compiler_params=pltpu.CompilerParams(vmem_limit_bytes=VMEM_LIMIT),
    )(x, og, gg, ug, h, gate_part, up_part, down_part, mixed, grad_input)


def body(inputs, gate_weight, up_weight, down_weight, out_grad):
    h, gg, ug, x, og, mixed, grad_input, gate_part, up_part, down_part = exchange(
        inputs, gate_weight, up_weight, down_weight, out_grad
    )
    width = inputs.shape[1]
    hidden = gate_weight.shape[1]
    return weight_grads(
        x.reshape(-1, width), og.reshape(-1, width),
        gg.reshape(-1, hidden), ug.reshape(-1, hidden), h.reshape(-1, hidden),
        gate_part, up_part, down_part, mixed, grad_input,
    )


def solution(mesh):
    in_specs = (P("row", "col"), P("col", "row"), P("col", "row"), P("row", "col"), P("row", "col"))
    out_specs = (
        P("row", "col"),
        P("row", "col"),
        P("col", "row"),
        P("col", "row"),
        P("row", "col"),
    )
    return jax.shard_map(body, mesh=mesh, in_specs=in_specs, out_specs=out_specs, check_vma=False)
```
